128 devices in a mesh: dp: 16 (over x, z), tensor: 8 (over y, core).
Axes of the slice: x: 4, y: 4, z: 4, core: 2. Of those that a mesh axis runs over, the one named last changes fastest.
Arguments:
- conv_input: bfloat16 [96, 96, 16384], P('dp', None, 'tensor'), may hold values from -6 to 6
- gate_input: bfloat16 [96, 96, 16384], P('dp', None, 'tensor'), may hold values from -6 to 6
- conv_weight: float32 [4, 16384], P(None, 'tensor'), may hold values from -3 to 3
- conv_bias: float32 [16384], P('tensor'), may hold values from -3 to 3
- state_pool: float32 [2048, 19456], P('dp', 'tensor'), may hold values from -6 to 6
- page_owner: int32 [96, 16, 1], P('dp'), may hold values from 0 to 15; in each aligned block of 96 rows (0 to 95, 96 to 191, ..., all dimensions but the last counted through in order) at most 9 rows name the same one
- page_slot: int32 [96, 16], P('dp'), may hold values from 0 to 127
- page_count: int32 [96], P('dp'), may hold values from 1 to 16
- step_in_weight: bfloat16 [16384, 512], P('tensor'), may hold values from -0.046875 to 0.046875
- coupling_weight: bfloat16 [32, 16384], P(None, 'tensor'), may hold values from -0.046875 to 0.046875
- step_gain: float32 [512], replicated, may hold values from 0.1 to 1.9
- step_weight: bfloat16 [512, 16384], P(None, 'tensor'), may hold values from -0.25 to 0.25
- step_bias: float32 [16384], P('tensor'), may hold values from -5 to -1
- decay_log: float32 [16, 16384], P(None, 'tensor'), may hold values from 0 to 2.8
- skip_gain: float32 [16384], P('tensor'), may hold values from 0.5 to 1.5
- out_weight: bfloat16 [16384, 4096], P('tensor', 'dp'), may hold values from -0.046875 to 0.046875
Outputs:
- mixer_out: bfloat16 [96, 96, 4096], P('dp', None, 'tensor')
- final_state: float32 [96, 16, 16384], P('dp', None, 'tensor')
The draws below stay inside these ranges and needn't reach their ends.
Inputs may be any that keep to these rules, and one draw needn't show every extreme that they name: `page_owner`: among the pages listed for the 6 sessions of one dp index, at most 9 name the same owner. `page_slot`: several pages may name the same row. `page_count`: pages at list positions from the count on were never stored and hold zero state, whatever the lists name there.
All inputs are finite; a program needn't handle non-finite values.
Results may differ from the reference program's by a relative error of at most 0.018.
Values may be sent and summed in bfloat16 or wider, within the bound.
A program may use at most 128 MiB of HBM per device.

```python
import math
import jax
import jax.numpy as jnp
import numpy as np
from jax import lax

DI = 16384
NS = 16
R = 512
KW = 4
D_OUT = 4096
PCH = 128
NEW = 96
S_DEV = 6
SESSIONS = 96
PAGES = 16
PAGE_LEN = 19456
SLOTS_DEV = 128
SLOTS = 2048
CAP = 9
N_DP = 16
N_TENSOR = 8


def plant(drawn, stream_key, smallest, top_value):
    longest = drawn.shape.index(max(drawn.shape))
    spots = []
    for shift in (0, 1):
        where = [jax.random.randint(jax.random.fold_in(stream_key, axis), (), 0, length) for axis, length in enumerate(drawn.shape)]
        where[longest] = (where[longest] + shift) % drawn.shape[longest]
        spots.append(tuple(where))
    return drawn.at[spots[0]].set(smallest).at[spots[1]].set(top_value)


def shard_levels(stream_key, extent, pieces, low, high):
    factor_of, own = 1.0, jax.random.fold_in(stream_key, 6)
    for dim, blocks in pieces:
        steps = jnp.exp(jax.random.uniform(jax.random.fold_in(own, dim), (blocks,), jnp.float32, low / len(pieces), high / len(pieces)))
        factor_of = factor_of * jnp.repeat(steps, extent[dim] // blocks).reshape([-1 if axis == dim else 1 for axis in range(len(extent))])
    return factor_of


def deal_out(key, own, number, rows, number_of, top, most, lean):
    order = jax.random.permutation(key, number_of)
    packed, ordinary = load_shares(number_of, rows * top, most, lean, True), load_shares(number_of, rows * top, most, lean, False)
    places = jnp.arange(number_of)

    def named(sizes, rotation):
        used = int((sizes > 0).sum())
        fixed = max(1, used // 4)
        moved = fixed + (places - fixed + rotation * (used - fixed)) % max(1, number_of - fixed)
        return jnp.zeros((number_of,), jnp.int32).at[order[jnp.where(places < fixed, places, moved)]].set(jnp.asarray(sizes, jnp.int32))

    sizes = jnp.where(number % 4 == 0, named(packed, number // 4), named(ordinary, number - number // 4 - 1))
    mixed = jax.random.permutation(jax.random.fold_in(own, 3), number_of)
    donor, taker = mixed[0:number_of // 2 * 2:2], mixed[1:number_of // 2 * 2:2]
    margin = jnp.minimum(sizes[donor] - 1, most - sizes[taker]) // 2
    margin = jnp.where((donor == order[0]) | (taker == order[0]) | (sizes[taker] == 0), 0, jnp.maximum(margin, 0))
    moved = jax.random.randint(jax.random.fold_in(own, 4), (number_of // 2,), 0, 1 << 20) % (margin + 1)
    sizes = sizes.at[donor].add(-moved).at[taker].add(moved)
    labels = jnp.searchsorted(jnp.cumsum(sizes), jnp.arange(rows * top), side="right").astype(jnp.int32)
    listing = labels.reshape(top, rows).T
    listing = listing[jax.random.permutation(jax.random.fold_in(own, 1), rows)]
    rotation = jax.random.randint(jax.random.fold_in(own, 2), (rows, 1), 0, top)
    return jnp.take_along_axis(listing, (jnp.arange(top)[None, :] + rotation) % top, axis=1)


def load_shares(count, total, limit, lean, full):
    weights = [(1 << 20) // math.isqrt(standing ** lean) + 1 for standing in range(1, count + 1)]
    largest = limit if full else min(limit, max(-(-total // count), total * weights[0] // sum(weights)))
    least = 1 if total - largest >= count - 1 else 0
    given, surplus = [largest] + [least] * (count - 1), total - largest - least * (count - 1)
    while surplus > 0:
        candidates = [i for i in range(1, count) if given[i] < largest] or [i for i in range(1, count) if given[i] < limit]
        mass, budget = sum([weights[i] for i in candidates]), surplus
        for i in candidates:
            more = min(limit - given[i], max(1, budget * weights[i] // mass), surplus)
            given[i] = given[i] + more
            surplus = surplus - more
    return np.array(given)


def noise(key, extent, width, bound, split=(), kind=jnp.bfloat16):
    level = shard_levels(key, extent, split, -0.22, 0.18) if split else 1.0
    values = jax.random.normal(key, extent, jnp.float32) * width * level
    return jnp.minimum(jnp.maximum(values, -bound), bound).astype(kind)


def setup_inputs(seed: int = 0) -> dict:
    key_of = jax.random.split(jax.random.key(seed), 17)
    conv_input = noise(key_of[0], (SESSIONS, NEW, DI), 1.0, 6.0, ((0, 16), (2, 8)))
    gate_input = noise(key_of[1], (SESSIONS, NEW, DI), 1.0, 6.0, ((0, 16), (2, 8)))
    conv_weight = noise(key_of[2], (KW, DI), 0.5, 3.0, ((1, 8),), jnp.float32)
    conv_bias = noise(key_of[3], (DI,), 0.5, 3.0, ((0, 8),), jnp.float32)
    state_pool = noise(key_of[4], (SLOTS, PAGE_LEN), 1.0, 6.0, ((0, 16), (1, 8)), jnp.float32)
    page_owner_keys = jax.random.split(jax.random.fold_in(key_of[5], 1), SESSIONS * PAGES // (S_DEV * PAGES))
    page_owner_turns = jax.random.permutation(jax.random.fold_in(key_of[5], 3), SESSIONS * PAGES // (S_DEV * PAGES))
    page_owner = jax.vmap(lambda own, number: deal_out(jax.random.fold_in(key_of[5], 2), own, number, S_DEV * PAGES, N_DP, 1, CAP, 2))(page_owner_keys, page_owner_turns).reshape((SESSIONS, PAGES, 1))
    page_slot = plant(jax.random.randint(key_of[6], (SESSIONS, PAGES), 0, SLOTS_DEV), jax.random.fold_in(key_of[6], 1), 0, SLOTS_DEV - 1).astype(jnp.int32)
    page_count = plant(jax.random.randint(key_of[7], (SESSIONS,), 1, PAGES + 1), jax.random.fold_in(key_of[7], 1), 1, PAGES).astype(jnp.int32)
    step_in_weight = noise(key_of[8], (DI, R), DI ** -0.5, 0.046875, ((0, 8),))
    coupling_weight = noise(key_of[9], (2 * NS, DI), DI ** -0.5, 0.046875, ((1, 8),))
    step_gain = jnp.clip(1.0 + 0.18 * jax.random.normal(key_of[10], (R,), jnp.float32), 0.1, 1.9)
    step_weight = noise(key_of[11], (R, DI), R ** -0.5, 0.25, ((1, 8),))
    step_bias = jnp.clip(-5.0 + 4.0 * jax.random.uniform(key_of[12], (DI,), jnp.float32) ** shard_levels(key_of[12], (DI,), ((0, 8),), -0.2, 0.2), -5.0, -1.0)
    decay_log = jnp.clip(2.8 * jax.random.uniform(key_of[13], (NS, DI), jnp.float32) ** shard_levels(key_of[13], (NS, DI), ((1, 8),), -0.2, 0.2), 0.0, 2.8)
    skip_gain = jnp.clip(0.5 + 1.0 * jax.random.uniform(key_of[14], (DI,), jnp.float32) ** shard_levels(key_of[14], (DI,), ((0, 8),), -0.2, 0.2), 0.5, 1.5)
    out_weight = noise(key_of[15], (DI, D_OUT), DI ** -0.5, 0.046875, ((0, 8), (1, 16)))
    return dict(conv_input=conv_input, gate_input=gate_input, conv_weight=conv_weight, conv_bias=conv_bias, state_pool=state_pool, page_owner=page_owner, page_slot=page_slot, page_count=page_count, step_in_weight=step_in_weight, coupling_weight=coupling_weight, step_gain=step_gain, step_weight=step_weight, step_bias=step_bias, decay_log=decay_log, skip_gain=skip_gain, out_weight=out_weight)


EPSILON = 1e-06

def reference(conv_input, gate_input, conv_weight, conv_bias, state_pool, page_owner, page_slot, page_count, step_in_weight, coupling_weight, step_gain, step_weight, step_bias, decay_log, skip_gain, out_weight):
    entry_width = NS + KW - 1
    wanted = page_owner[:, :, 0] * SLOTS_DEV + page_slot
    fetched = state_pool[wanted]
    stored = (jnp.arange(PAGES, dtype=jnp.int32)[None, :] < page_count[:, None]).astype(jnp.float32)
    fetched = fetched * stored[:, :, None]
    fetched = fetched.reshape(SESSIONS, PAGES, N_TENSOR, PCH, entry_width)
    unpacked = jnp.transpose(fetched, (0, 4, 2, 1, 3)).reshape(SESSIONS, entry_width, DI)
    start_state = unpacked[:, :NS]
    conv_history = unpacked[:, NS:]
    decay_rate = -jnp.exp(decay_log)
    weight_blocks = out_weight.astype(jnp.float32).reshape(N_TENSOR, DI // N_TENSOR, D_OUT)

    def session(inputs):
        signal_in, gate_in, state_in, history_in = inputs
        history = jnp.concatenate([history_in, signal_in.astype(jnp.float32)], axis=0)
        pre_act = conv_bias
        for tap_index in range(KW):
            pre_act = pre_act + conv_weight[tap_index] * history[tap_index:tap_index + NEW]
        signal = jax.nn.silu(pre_act)
        signal_low = signal.astype(jnp.bfloat16)
        step_low = jnp.dot(signal_low, step_in_weight, preferred_element_type=jnp.float32)
        coupling = jnp.dot(signal_low, coupling_weight.T, preferred_element_type=jnp.float32)
        inv_rms = lax.rsqrt(lax.optimization_barrier(jnp.mean(step_low * step_low, axis=-1, keepdims=True)) + EPSILON)
        step_normed = (step_low * inv_rms * step_gain).astype(jnp.bfloat16)
        step_size = jax.nn.softplus(jnp.dot(step_normed, step_weight, preferred_element_type=jnp.float32) + step_bias)

        def advance(carried, inputs_now):
            step_now, signal_now, b_now, c_now = inputs_now
            carried = jnp.exp(step_now[None, :] * decay_rate) * carried + (step_now * signal_now)[None, :] * b_now[:, None]
            result = lax.optimization_barrier(jnp.sum(c_now[:, None] * carried, axis=0)) + skip_gain * signal_now
            return (carried, result)
        final_one, outputs = lax.scan(advance, state_in, (step_size, signal, coupling[:, :NS], coupling[:, NS:]))
        gated_out = (outputs * jax.nn.silu(gate_in.astype(jnp.float32))).astype(jnp.bfloat16)
        blocks = gated_out.astype(jnp.float32).reshape(NEW, N_TENSOR, DI // N_TENSOR)
        partials = jnp.einsum('tjc,jcd->jtd', blocks, weight_blocks)
        partials = lax.optimization_barrier(partials.astype(jnp.bfloat16)).astype(jnp.float32)
        return (lax.optimization_barrier(jnp.sum(partials, axis=0)).astype(jnp.bfloat16), final_one)
    mixer_out, final_state = lax.map(session, (conv_input, gate_input, start_state, conv_history))
    return (mixer_out, final_state)
```

```python
import jax
import jax.numpy as jnp
from jax import lax
from jax.experimental import pallas as pl
from jax.experimental.pallas import tpu as pltpu
from jax.sharding import PartitionSpec as P

EPSILON = 1e-06
LOG2E = 1.4426950408889634
MESH = pl.DeviceIdType.MESH
F32 = jnp.float32
BF16 = jnp.bfloat16

SESS, NEW, ROWS = 6, 96, 576
CB, LANES, CH = 16, 128, 2048
NS, KW, RANK, ENT = 16, 4, 512, 19
PAGE = CH // CB * ENT
HALF = 10 * LANES
RB = 80
PW = RANK + LANES
QR = 1024


def gather_label(q, da, db, p):
    return ((q * 4 + da) * 4 + db) * 2 + p


def gather_events():
    groups = (
        [(0, 0)],
        [(1, 0), (3, 0)],
        [(0, 1), (0, 3), (2, 0)],
        [(1, 1), (1, 3), (3, 1), (3, 3)],
        [(0, 2)],
        [(2, 1), (2, 3)],
        [(1, 2), (3, 2)],
        [(2, 2)],
    )
    return [(q, da, db, p) for g in groups for (da, db) in g for p in (0, 1) for q in (0, 1)]


def gather_forwards(q, da, db, p):
    out = []
    if db == 0:
        if da == 0:
            out += [("a", 1, (q, 1, 0, p)), ("a", 3, (q, 3, 0, p))]
        if da == 1 and p == 0:
            out.append(("a", 1, (q, 2, 0, 0)))
        if da == 3 and p == 1:
            out.append(("a", 3, (q, 2, 0, 1)))
        out += [("b", 1, (q, da, 1, p)), ("b", 3, (q, da, 3, p))]
    else:
        if db == 1 and p == 0:
            out.append(("b", 1, (q, da, 2, 0)))
        if db == 3 and p == 1:
            out.append(("b", 3, (q, da, 2, 1)))
    return out


def sigmoid(v):
    return 0.5 * (1.0 + jnp.tanh(0.5 * v))


def dot_nt(a, b):
    return lax.dot_general(a, b, (((1,), (1,)), ((), ())), preferred_element_type=F32)


def dot(a, b):
    return jnp.dot(a, b, preferred_element_type=F32)


def iota(shape, dim):
    return lax.broadcasted_iota(jnp.int32, shape, dim)


def kernel(
    conv_w, conv_b, meta, coup_w, step_gain, step_b, decay_log, skip,
    conv_in, gate_in, pool, step_in_w, step_w, out_w,
    mixer_out, final_state,
    W, G, XN, GN, SIW, SWV, S2, D2, PL, PP, REQ, RQIN, PS, PRV, S8, P8, RALL, FT,
    SPB, CPW, RSS, RSR, AGB, EB, BC, FSB, FSV, OB, RBO, OUTV,
    loc_sem, ag_send, ag_recv, sib_send, sib_recv, rq_send, rq_recv,
    pa_send, pa_recv, pb_send, pb_recv, rs_send, rs_recv, an_send, an_recv,
    gx_send, gx_recv, ob_send, ob_recv, fs_sem,
):
    dp = lax.axis_index("dp")
    tn = lax.axis_index("tensor")
    x, z = dp // 4, dp % 4
    core = tn % 2
    sib = tn + 1 - 2 * core
    sends = []

    def remote(src, dst, ssem, rsem, to):
        c = pltpu.make_async_remote_copy(
            src_ref=src, dst_ref=dst, send_sem=ssem, recv_sem=rsem,
            device_id=to, device_id_type=MESH,
        )
        c.start()
        sends.append(c)

    def arrived(ref, ssem, rsem):
        pltpu.make_async_remote_copy(
            src_ref=ref, dst_ref=ref, send_sem=ssem, recv_sem=rsem,
            device_id=(dp, tn), device_id_type=MESH,
        ).wait_recv()

    def local(src, dst, k):
        c = pltpu.make_async_copy(src, dst, loc_sem.at[k])
        c.start()
        return c

    own_rows = pl.multiple_of(core * CH, CH)
    sib_rows = pl.multiple_of(CH - core * CH, CH)
    own_lanes = pl.multiple_of(core * LANES, LANES)
    sib_lanes = pl.multiple_of(LANES - core * LANES, LANES)
    ld_w = local(out_w.at[:, pl.ds(own_lanes, LANES)], W.at[dp, pl.ds(own_rows, CH)], 0)
    ld_pool = local(pool, PL, 1)
    ld_x = local(conv_in, XN, 2)
    ld_siw = local(step_in_w, SIW, 3)
    ld_sw = local(step_w, SWV, 4)
    ld_g = local(gate_in, GN, 5)

    bar = pltpu.get_barrier_semaphore()
    for d in range(1, 16):
        pl.semaphore_signal(bar, inc=1, device_id=((dp + d) % 16, tn), device_id_type=MESH)
    for d in range(1, 8):
        pl.semaphore_signal(bar, inc=1, device_id=(dp, (tn + d) % 8), device_id_type=MESH)
    pl.semaphore_wait(bar, 22)

    def part_rows(q, p):
        base = own_rows if q == 0 else sib_rows
        return pl.ds(pl.multiple_of(base + p * QR, QR), QR)

    def dp_of(q, a, b):
        return a * 4 + b if q == 0 else b * 4 + a

    def coords(q):
        return (x, z) if q == 0 else (z, x)

    def part(q, da, db, p):
        a, b = coords(q)
        return W.at[dp_of(q, (a + 4 - da) % 4, (b + 4 - db) % 4), part_rows(q, p)]

    def gather_step(label):
        q, da, db, p = label
        a, b = coords(q)
        ref = part(q, da, db, p)
        if (da, db) != (0, 0):
            k = gather_label(*label)
            arrived(ref, ag_send.at[k], ag_recv.at[k])
        elif q == 1:
            arrived(ref, sib_send.at[p], sib_recv.at[p])
        for axis, step, nlabel in gather_forwards(*label):
            k = gather_label(*nlabel)
            to = ((a + step) % 4, b) if axis == "a" else (a, (b + step) % 4)
            remote(ref, ref, ag_send.at[k], ag_recv.at[k], (dp_of(q, *to), tn))

    events = gather_events()
    cursor = [0]

    def advance(upto):
        while cursor[0] < min(upto, len(events)):
            gather_step(events[cursor[0]])
            cursor[0] += 1

    for p in (0, 1):
        remote(
            out_w.at[pl.ds(p * QR, QR), pl.ds(sib_lanes, LANES)],
            W.at[dp, part_rows(0, p)], sib_send.at[p], sib_recv.at[p], (dp, sib),
        )

    owner, slot, stored = meta[0:1, :], meta[1:2, :], meta[2:3, :]
    own_hot = (owner == iota((16, LANES), 0)).astype(F32)
    before = (iota((LANES, LANES), 0) < iota((LANES, LANES), 1)).astype(F32).astype(BF16)
    ahead = dot(own_hot.astype(BF16), before)
    rank = jnp.sum(own_hot * ahead, axis=0, keepdims=True).astype(jnp.int32)
    ask_row = jnp.where(stored > 0, owner * 16 + rank, -1)
    got_row = jnp.where(stored > 0, jnp.where(rank < 8, owner * 8 + rank, LANES + owner), -1)
    row_io = iota((256, LANES), 0)
    ask = (ask_row == row_io).astype(F32).astype(BF16)
    slot_hot = (iota((LANES, LANES), 0) == slot).astype(F32).astype(BF16)
    REQ[...] = dot_nt(ask, slot_hot).astype(BF16).reshape(16, 16, LANES)
    RQIN[dp] = REQ[dp]
    for d in range(1, 16):
        to = (dp + d) % 16
        remote(REQ.at[to], RQIN.at[dp], rq_send.at[d], rq_recv.at[d], (to, tn))
    got = (got_row == row_io).astype(F32).T[0:96, :].astype(BF16)

    ld_w.wait()
    advance(4)

    ld_pool.wait()
    pool_low = PL[...].astype(BF16)

    def permute(e, _):
        pick = (iota((PAGE, LANES), 0) - ENT * iota((PAGE, LANES), 1) == e).astype(F32)
        PP[:, pl.ds(pl.multiple_of(e * LANES, LANES), LANES)] = dot(
            pool_low, pick.astype(BF16)
        ).astype(BF16)
        return 0

    lax.fori_loop(0, ENT, permute, 0)
    PP[:, ENT * LANES :] = jnp.zeros((LANES, LANES), BF16)

    for d in range(1, 16):
        src = (dp + 16 - d) % 16
        arrived(RQIN.at[src], rq_send.at[d], rq_recv.at[d])
    asked = RQIN[...].astype(F32)
    first8 = asked[:, 0:8, :].reshape(LANES, LANES).astype(BF16)
    low = dot(first8, PP[:, 0:HALF]).reshape(16, 8, HALF)
    high = dot(first8, PP[:, HALF : 2 * HALF]).reshape(16, 8, HALF)
    PS[...] = jnp.concatenate([low, high], axis=1).astype(BF16)
    ninth = dot(asked[:, 8, :].astype(BF16), PP[...])
    S8[...] = ninth.reshape(16, 1, 2 * HALF)
    PRV[dp] = PS[dp]
    P8[dp] = S8[dp]
    for d in range(1, 16):
        to = (dp + d) % 16
        remote(PS.at[to], PRV.at[dp], pa_send.at[d], pa_recv.at[d], (to, tn))
        remote(S8.at[to], P8.at[dp], pb_send.at[d], pb_recv.at[d], (to, tn))

    for p in range(CB):
        cols = slice(p * LANES, (p + 1) * LANES)
        SPB[pl.ds(p, KW, stride=CB), :] = conv_w[:, cols]
        SPB[pl.ds(4 * CB + p, 1), :] = conv_b[:, cols]
        SPB[pl.ds(5 * CB + p, 1), :] = skip[:, cols]
        SPB[pl.ds(8 * CB + p, NS, stride=CB), :] = -LOG2E * jnp.exp(decay_log[:, cols])
    EB[...] = (iota((LANES, 2 * NS * LANES), 0) == iota((LANES, 2 * NS * LANES), 1) // LANES).astype(
        F32
    ).astype(BF16)
    CPW[...] = jnp.zeros_like(CPW)
    CPW[0 : 2 * NS, :] = coup_w[...]
    RSS[ROWS:, :] = jnp.zeros((8 * RB - ROWS, PW), BF16)

    ld_x.wait()

    def spread(g, _):
        r = pl.multiple_of(g * 16, 16)
        for p in range(CB):
            S2[pl.ds(g * 256 + p, 16, stride=CB), :] = XN[
                pl.ds(r, 16), p * LANES : (p + 1) * LANES
            ].astype(F32)
        return 0

    lax.fori_loop(0, ROWS // 16, spread, 0)

    for d in range(1, 16):
        src = (dp + 16 - d) % 16
        arrived(PRV.at[src], pa_send.at[d], pa_recv.at[d])
        arrived(P8.at[src], pb_send.at[d], pb_recv.at[d])

    for s in range(2):
        for o in range(16):
            RALL[o * 8 : o * 8 + 8, :] = PRV[o].astype(F32)[8 * s : 8 * s + 8, :]
        RALL[LANES : LANES + 16, :] = P8[...].reshape(16, 2 * HALF)[:, s * HALF : (s + 1) * HALF]
        RALL[LANES + 16 :, :] = jnp.zeros((LANES - 16, HALF), F32)
        FT[:, s * HALF : (s + 1) * HALF] = dot(got, RALL[...].astype(BF16))

    taps = [SPB[w * CB : (w + 1) * CB, :] for w in range(KW)]
    bias = SPB[4 * CB : 5 * CB, :]

    def conv_session(s, _):
        def old(w):
            return FT[
                pl.ds(pl.multiple_of(s * CB, CB), CB), (NS + w) * LANES : (NS + w + 1) * LANES
            ]

        def step(i, hist):
            h3, h2, h1 = hist
            for u in range(8):
                at = pl.ds(pl.multiple_of((s * NEW + i * 8 + u) * CB, CB), CB)
                now = S2[at, :]
                pre = bias + taps[0] * h3 + taps[1] * h2 + taps[2] * h1 + taps[3] * now
                S2[at, :] = pre * sigmoid(pre)
                h3, h2, h1 = h2, h1, now
            return (h3, h2, h1)

        lax.fori_loop(0, NEW // 8, step, (old(0), old(1), old(2)))
        return 0

    lax.fori_loop(0, SESS, conv_session, 0)

    def collect(g, _):
        r = pl.multiple_of(g * 16, 16)
        for p in range(CB):
            XN[pl.ds(r, 16), p * LANES : (p + 1) * LANES] = S2[
                pl.ds(g * 256 + p, 16, stride=CB), :
            ].astype(BF16)
        return 0

    lax.fori_loop(0, ROWS // 16, collect, 0)

    ld_siw.wait()

    def project(m, _):
        r = pl.ds(pl.multiple_of(m * 96, 96), 96)
        RSS[r, 0:RANK] = dot(XN[r, :], SIW[...]).astype(BF16)
        RSS[r, RANK:] = dot_nt(XN[r, :], CPW[...]).astype(BF16)
        return 0

    lax.fori_loop(0, ROWS // 96, project, 0)
    for d in range(1, 8):
        to = (tn + d) % 8
        remote(
            RSS.at[pl.ds(pl.multiple_of(to * RB, 16), RB)], RSR.at[d],
            rs_send.at[d], rs_recv.at[d], (dp, to),
        )
    advance(8)
    mine = pl.ds(pl.multiple_of(tn * RB, 16), RB)
    total = RSS[mine, :].astype(F32)
    for d in range(1, 8):
        arrived(RSR.at[d], rs_send.at[d], rs_recv.at[d])
        total = total + RSR[d].astype(F32)
    step_low = total[:, 0:RANK]
    inv_rms = lax.rsqrt(jnp.mean(step_low * step_low, axis=-1, keepdims=True) + EPSILON)
    AGB[mine, 0:RANK] = (step_low * inv_rms * step_gain[...]).astype(BF16)
    AGB[mine, RANK:] = total[:, RANK:].astype(BF16)
    for d in range(1, 8):
        to = (tn + d) % 8
        remote(AGB.at[mine], AGB.at[mine], an_send.at[d], an_recv.at[d], (dp, to))
    advance(16)
    for d in range(1, 8):
        src = (tn + 8 - d) % 8
        arrived(
            AGB.at[pl.ds(pl.multiple_of(src * RB, 16), RB)], an_send.at[d], an_recv.at[d]
        )

    ld_sw.wait()

    def step_size(m, _):
        r = pl.ds(pl.multiple_of(m * 96, 96), 96)
        for p in range(0, CB, 2):
            cols = slice(p * LANES, (p + 2) * LANES)
            v = dot(AGB[r, 0:RANK], SWV[:, cols]) + step_b[:, cols]
            v = jnp.maximum(v, 0.0) + jnp.log1p(jnp.exp(-jnp.abs(v)))
            for i in (0, 1):
                D2[pl.ds(m * 96 * CB + p + i, 96, stride=CB), :] = v[:, i * LANES : (i + 1) * LANES]
        return 0

    lax.fori_loop(0, ROWS // 96, step_size, 0)
    advance(20)

    ld_g.wait()
    outs = []
    for s in range(SESS):
        both = dot(AGB[s * NEW : (s + 1) * NEW, RANK:], EB[...])
        for n in range(2 * NS):
            BC[n * NEW : (n + 1) * NEW, :] = both[:, n * LANES : (n + 1) * LANES]
        for h in (0, 1):
            rate = [SPB[(8 + n) * CB + 8 * h : (8 + n) * CB + 8 * h + 8, :] for n in range(NS)]
            direct = SPB[5 * CB + 8 * h : 5 * CB + 8 * h + 8, :]
            start = tuple(
                FT[s * CB + 8 * h : s * CB + 8 * h + 8, n * LANES : (n + 1) * LANES]
                for n in range(NS)
            )

            def token(i, state, h=h, s=s, rate=rate, direct=direct):
                state = list(state)
                for u in range(4):
                    t = i * 4 + u
                    at = pl.ds(pl.multiple_of((s * NEW + t) * CB + 8 * h, 8), 8)
                    dt, sg = D2[at, :], S2[at, :]
                    dx = dt * sg
                    acc = [direct * sg, None]
                    for n in range(NS):
                        bn = BC[pl.ds(n * NEW + t, 8, stride=0), :]
                        cn = BC[pl.ds((NS + n) * NEW + t, 8, stride=0), :]
                        state[n] = jnp.exp2(dt * rate[n]) * state[n] + dx * bn
                        term = cn * state[n]
                        acc[n % 2] = term if acc[n % 2] is None else acc[n % 2] + term
                    S2[at, :] = acc[0] + acc[1]
                return tuple(state)

            last = lax.fori_loop(0, NEW // 4, token, start)
            for n in range(NS):
                FSB[n * CB + 8 * h : n * CB + 8 * h + 8, :] = last[n]
        for p in range(CB):
            FSV[s, :, p * LANES : (p + 1) * LANES] = FSB[pl.ds(p, NS, stride=CB), :]
        c = pltpu.make_async_copy(FSV.at[s], final_state.at[s], fs_sem.at[s])
        c.start()
        outs.append(c)

        def gate(g, _, s=s):
            r = pl.ds(pl.multiple_of(s * NEW + g * 16, 16), 16)
            for p in range(CB):
                cols = slice(p * LANES, (p + 1) * LANES)
                gt = GN[r, cols].astype(F32)
                y = S2[pl.ds((s * NEW + g * 16) * CB + p, 16, stride=CB), :]
                G[core, r, cols] = (y * (gt * sigmoid(gt))).astype(BF16)
            return 0

        lax.fori_loop(0, NEW // 16, gate, 0)
        here = G.at[core, pl.ds(s * NEW, NEW)]
        remote(here, here, gx_send.at[s], gx_recv.at[s], (dp, sib))
        advance(20 + 6 * (s + 1))

    for s in range(SESS):
        arrived(G.at[1 - core, pl.ds(s * NEW, NEW)], gx_send.at[s], gx_recv.at[s])

    def multiply(dx, dz):
        src = ((x + 4 - dx) % 4) * 4 + (z + 4 - dz) % 4
        to, side = src // 2, src % 2

        def rows(m, _):
            r = pl.ds(pl.multiple_of(m * 192, 192), 192)
            v = dot(G[0, r, :], W[src, 0:CH, :]) + dot(G[1, r, :], W[src, CH : 2 * CH, :])
            OB[src, r, :] = v.astype(BF16)
            return 0

        lax.fori_loop(0, ROWS // 192, rows, 0)

        @pl.when(to != tn)
        def _():
            c = pltpu.make_async_remote_copy(
                src_ref=OB.at[src], dst_ref=RBO.at[tn, side], send_sem=ob_send.at[src],
                recv_sem=ob_recv.at[tn, side], device_id=(dp, to), device_id_type=MESH,
            )
            c.start()

        @pl.when(to == tn)
        def _():
            RBO[tn, side] = OB[src]

    seen = {}
    for i, (q, da, db, p) in enumerate(events):
        key = (da, db) if q == 0 else (db, da)
        seen[key] = max(seen.get(key, 0), i)
    for key in sorted(seen, key=lambda k: seen[k]):
        advance(seen[key] + 1)
        multiply(*key)
    advance(len(events))

    for d in range(8):
        src = (tn + 8 - d) % 8
        for side in (0, 1):
            if d:
                arrived(RBO.at[src, side], ob_send.at[0], ob_recv.at[src, side])
    for c in (0, 1):
        for side in (0, 1):
            cols = slice(side * 256 + c * LANES, side * 256 + (c + 1) * LANES)

            def finish(m, _, c=c, side=side, cols=cols):
                r = pl.ds(pl.multiple_of(m * 96, 96), 96)
                v = RBO[c, side, r, :].astype(F32)
                for y in range(1, 4):
                    v = v + RBO[2 * y + c, side, r, :].astype(F32)
                OUTV[r, cols] = v.astype(BF16)
                return 0

            lax.fori_loop(0, ROWS // 96, finish, 0)
    c = pltpu.make_async_copy(OUTV, mixer_out, fs_sem.at[SESS])
    c.start()
    outs.append(c)
    for src in range(16):

        @pl.when(src // 2 != tn)
        def _(src=src):
            pltpu.make_async_remote_copy(
                src_ref=OB.at[src], dst_ref=OB.at[src], send_sem=ob_send.at[src],
                recv_sem=ob_recv.at[0, 0], device_id=(dp, tn), device_id_type=MESH,
            ).wait_send()

    for c in sends:
        c.wait_send()
    for c in outs:
        c.wait()


def body(
    conv_input, gate_input, conv_weight, conv_bias, state_pool, page_owner, page_slot, page_count,
    step_in_weight, coupling_weight, step_gain, step_weight, step_bias, decay_log, skip_gain,
    out_weight,
):
    pages = page_slot.shape[1]
    stored = jnp.arange(pages, dtype=jnp.int32)[None, :] < page_count[:, None]
    rows = jnp.stack(
        [page_owner[:, :, 0].reshape(-1), page_slot.reshape(-1), stored.astype(jnp.int32).reshape(-1)]
    )
    meta = jnp.pad(rows, ((0, 5), (0, LANES - rows.shape[1])), constant_values=-1)
    vmem = pl.BlockSpec(memory_space=pltpu.VMEM)
    hbm = pl.BlockSpec(memory_space=pl.ANY)
    sem = pltpu.SemaphoreType.DMA
    mixer_out, final_state = pl.pallas_call(
        kernel,
        out_shape=(
            jax.ShapeDtypeStruct((ROWS, 512), BF16),
            jax.ShapeDtypeStruct((SESS, NS, CH), F32),
        ),
        in_specs=[vmem] * 8 + [hbm] * 6,
        out_specs=(hbm, hbm),
        scratch_shapes=[
            pltpu.VMEM((16, 2 * CH, LANES), BF16),
            pltpu.VMEM((2, ROWS, CH), BF16),
            pltpu.VMEM((ROWS, CH), BF16),
            pltpu.VMEM((ROWS, CH), BF16),
            pltpu.VMEM((CH, RANK), BF16),
            pltpu.VMEM((RANK, CH), BF16),
            pltpu.VMEM((ROWS * CB, LANES), F32),
            pltpu.VMEM((ROWS * CB, LANES), F32),
            pltpu.VMEM((LANES, PAGE), F32),
            pltpu.VMEM((LANES, 2 * HALF), BF16),
            pltpu.VMEM((16, 16, LANES), BF16),
            pltpu.VMEM((16, 16, LANES), BF16),
            pltpu.VMEM((16, 16, HALF), BF16),
            pltpu.VMEM((16, 16, HALF), BF16),
            pltpu.VMEM((16, 1, 2 * HALF), F32),
            pltpu.VMEM((16, 1, 2 * HALF), F32),
            pltpu.VMEM((256, HALF), F32),
            pltpu.VMEM((96, 2 * HALF), F32),
            pltpu.VMEM((24 * CB, LANES), F32),
            pltpu.VMEM((LANES, CH), BF16),
            pltpu.VMEM((8 * RB, PW), BF16),
            pltpu.VMEM((8, RB, PW), BF16),
            pltpu.VMEM((8 * RB, PW), BF16),
            pltpu.VMEM((LANES, 2 * NS * LANES), BF16),
            pltpu.VMEM((2 * NS * NEW, LANES), F32),
            pltpu.VMEM((NS * CB, LANES), F32),
            pltpu.VMEM((SESS, NS, CH), F32),
            pltpu.VMEM((16, ROWS, LANES), BF16),
            pltpu.VMEM((8, 2, ROWS, LANES), BF16),
            pltpu.VMEM((ROWS, 512), BF16),
            sem((6,)), sem((64,)), sem((64,)), sem((2,)), sem((2,)), sem((16,)), sem((16,)),
            sem((16,)), sem((16,)), sem((16,)), sem((16,)), sem((8,)), sem((8,)), sem((8,)), sem((8,)),
            sem((SESS,)), sem((SESS,)), sem((16,)), sem((8, 2)), sem((SESS + 1,)),
        ],
        compiler_params=pltpu.CompilerParams(
            collective_id=0, has_side_effects=True, vmem_limit_bytes=62 << 20
        ),
        cost_estimate=pl.CostEstimate(
            flops=2 * ROWS * CH * (4096 + 1056), bytes_accessed=12 << 20, transcendentals=20 << 20
        ),
    )(
        conv_weight, conv_bias.reshape(1, -1), meta, coupling_weight, step_gain.reshape(1, -1),
        step_bias.reshape(1, -1), decay_log, skip_gain.reshape(1, -1),
        conv_input.reshape(ROWS, CH), gate_input.reshape(ROWS, CH), state_pool,
        step_in_weight, step_weight, out_weight,
    )
    return mixer_out.reshape(SESS, NEW, 512), final_state


def solution(mesh):
    return jax.shard_map(
        body,
        mesh=mesh,
        in_specs=(
            P("dp", None, "tensor"),
            P("dp", None, "tensor"),
            P(None, "tensor"),
            P("tensor"),
            P("dp", "tensor"),
            P("dp", None, None),
            P("dp", None),
            P("dp"),
            P("tensor", None),
            P(None, "tensor"),
            P(),
            P(None, "tensor"),
            P("tensor"),
            P(None, "tensor"),
            P("tensor"),
            P("tensor", "dp"),
        ),
        out_specs=(P("dp", None, "tensor"), P("dp", None, "tensor")),
        check_vma=False,
    )
```

```python
import jax
import jax.numpy as jnp
from jax import lax
from jax.experimental import pallas as pl
from jax.experimental.pallas import tpu as pltpu
from jax.sharding import PartitionSpec as P

EPSILON = 1e-06
LOG2E = 1.4426950408889634
MESH = pl.DeviceIdType.MESH
F32 = jnp.float32
BF16 = jnp.bfloat16

SESS, NEW, ROWS = 6, 96, 576
CB, LANES, CH = 16, 128, 2048
NS, KW, RANK, ENT = 16, 4, 512, 19
PAGE = CH // CB * ENT
HALF = 10 * LANES
RB = 80
PW = RANK + LANES
FIX = 32
QR = 1024


def gather_label(q, da, db, p):
    return ((q * 4 + da) * 4 + db) * 2 + p


def gather_events():
    return [
        (0, 0, 0, 0), (0, 0, 0, 1), (1, 0, 0, 0), (1, 0, 0, 1),
        (0, 0, 1, 0), (0, 0, 3, 0), (0, 1, 0, 0), (0, 3, 0, 0),
        (0, 0, 3, 1), (0, 0, 1, 1), (0, 1, 0, 1), (0, 3, 0, 1),
        (1, 1, 0, 0), (1, 0, 3, 0), (1, 0, 1, 0), (1, 3, 0, 0),
        (1, 0, 3, 1), (1, 0, 1, 1), (1, 3, 0, 1), (1, 1, 0, 1),
        (0, 1, 3, 0), (0, 2, 0, 0), (0, 2, 0, 1), (0, 0, 2, 0),
        (0, 1, 1, 0), (0, 3, 3, 0), (1, 1, 3, 0), (1, 1, 1, 0),
        (0, 3, 1, 0), (1, 3, 3, 0), (1, 0, 2, 0), (0, 0, 2, 1),
        (1, 3, 1, 0), (0, 1, 1, 1), (0, 1, 3, 1), (1, 0, 2, 1),
        (1, 3, 1, 1), (1, 3, 3, 1), (0, 3, 1, 1), (0, 3, 3, 1),
        (1, 1, 1, 1), (1, 1, 3, 1), (1, 2, 0, 1), (1, 2, 0, 0),
        (0, 2, 1, 0), (0, 2, 3, 0), (1, 1, 2, 0), (1, 3, 2, 1),
        (0, 2, 1, 1), (0, 2, 3, 1), (1, 3, 2, 0), (1, 1, 2, 1),
        (1, 2, 3, 1), (1, 2, 1, 1), (0, 1, 2, 1), (0, 1, 2, 0),
        (1, 2, 1, 0), (1, 2, 3, 0), (0, 3, 2, 1), (0, 3, 2, 0),
        (0, 2, 2, 0), (0, 2, 2, 1), (1, 2, 2, 1), (1, 2, 2, 0),
    ]


PAIRS = (
    ((0, 0), (0, 1)), ((0, 3), (1, 0)), ((3, 0), (2, 0)), ((1, 3), (3, 3)),
    ((1, 1), (3, 1)), ((0, 2), (2, 1)), ((2, 3), (1, 2)), ((3, 2), (2, 2)),
)
EARLY = 2
HROWS = ROWS // 2


def gather_forwards(q, da, db, p):
    out = []
    if db == 0:
        if da == 0:
            out += [("a", 1, (q, 1, 0, p)), ("a", 3, (q, 3, 0, p))]
        if da == 1 and p == 0:
            out.append(("a", 1, (q, 2, 0, 0)))
        if da == 3 and p == 1:
            out.append(("a", 3, (q, 2, 0, 1)))
        out += [("b", 1, (q, da, 1, p)), ("b", 3, (q, da, 3, p))]
    else:
        if db == 1 and p == 0:
            out.append(("b", 1, (q, da, 2, 0)))
        if db == 3 and p == 1:
            out.append(("b", 3, (q, da, 2, 1)))
    return out


def sigmoid(v):
    return 0.5 * (1.0 + jnp.tanh(0.5 * v))


def dot_nt(a, b):
    return lax.dot_general(a, b, (((1,), (1,)), ((), ())), preferred_element_type=F32)


def dot(a, b):
    return jnp.dot(a, b, preferred_element_type=F32)


def iota(shape, dim):
    return lax.broadcasted_iota(jnp.int32, shape, dim)


def kernel(
    page_owner, page_slot, page_count, conv_w, conv_b, coup_w, step_gain, step_b, decay_log, skip,
    conv_in, gate_in, pool, step_in_w, step_w, out_w,
    mixer_out, final_state,
    W, G, XN, GN, SIW, SWV, S2, D2, PL, PP, REQ, RQIN, PS, PRV, S8, P8, RALL, FT,
    PRE, F2, XF, FXS, FXR,
    SPB, CPW, RSS, RSR, AGB, EB, BC, FSB, FSV, OB, RBO, OUTV,
    loc_sem, ag_send, ag_recv, sib_send, sib_recv, rq_send, rq_recv,
    pa_send, pa_recv, pb_send, pb_recv, rs_send, rs_recv, an_send, an_recv, fx_send, fx_recv,
    gx_send, gx_recv, ob_send, ob_recv, fs_sem, out_sem,
):
    dp = lax.axis_index("dp")
    tn = lax.axis_index("tensor")
    x, z = dp // 4, dp % 4
    core = tn % 2
    sib = tn + 1 - 2 * core
    sends = []

    def remote(src, dst, ssem, rsem, to, kept=sends):
        c = pltpu.make_async_remote_copy(
            src_ref=src, dst_ref=dst, send_sem=ssem, recv_sem=rsem,
            device_id=to, device_id_type=MESH,
        )
        c.start()
        kept.append(c)

    def arrived(ref, ssem, rsem):
        pltpu.make_async_remote_copy(
            src_ref=ref, dst_ref=ref, send_sem=ssem, recv_sem=rsem,
            device_id=(dp, tn), device_id_type=MESH,
        ).wait_recv()

    def local(src, dst, k):
        c = pltpu.make_async_copy(src, dst, loc_sem.at[k])
        c.start()
        return c

    own_rows = pl.multiple_of(core * CH, CH)
    sib_rows = pl.multiple_of(CH - core * CH, CH)
    own_lanes = pl.multiple_of(core * LANES, LANES)
    sib_lanes = pl.multiple_of(LANES - core * LANES, LANES)
    ld_w = local(out_w.at[:, pl.ds(own_lanes, LANES)], W.at[dp, pl.ds(own_rows, CH)], 0)
    ld_pool = local(pool, PL, 1)
    ld_x = local(conv_in, XN, 2)
    ld_siw = local(step_in_w, SIW, 3)
    ld_sw = local(step_w, SWV, 4)
    ld_g = local(gate_in, GN, 5)

    bar = pltpu.get_barrier_semaphore()
    for d in range(1, 16):
        pl.semaphore_signal(bar, inc=1, device_id=((dp + d) % 16, tn), device_id_type=MESH)
    for d in range(1, 8):
        pl.semaphore_signal(bar, inc=1, device_id=(dp, (tn + d) % 8), device_id_type=MESH)
    pl.semaphore_wait(bar, 22)

    def part_rows(q, p):
        base = own_rows if q == 0 else sib_rows
        return pl.ds(pl.multiple_of(base + p * QR, QR), QR)

    def dp_of(q, a, b):
        return a * 4 + b if q == 0 else b * 4 + a

    def coords(q):
        return (x, z) if q == 0 else (z, x)

    def part(q, da, db, p):
        a, b = coords(q)
        return W.at[dp_of(q, (a + 4 - da) % 4, (b + 4 - db) % 4), part_rows(q, p)]

    def gather_step(label):
        q, da, db, p = label
        a, b = coords(q)
        ref = part(q, da, db, p)
        if (da, db) != (0, 0):
            k = gather_label(*label)
            arrived(ref, ag_send.at[k], ag_recv.at[k])
        elif q == 1:
            arrived(ref, sib_send.at[p], sib_recv.at[p])
        for axis, step, nlabel in gather_forwards(*label):
            k = gather_label(*nlabel)
            to = ((a + step) % 4, b) if axis == "a" else (a, (b + step) % 4)
            remote(ref, ref, ag_send.at[k], ag_recv.at[k], (dp_of(q, *to), tn))

    events = gather_events()
    cursor = [0]

    def advance(upto):
        while cursor[0] < min(upto, len(events)):
            gather_step(events[cursor[0]])
            cursor[0] += 1

    for p in (0, 1):
        remote(
            out_w.at[pl.ds(p * QR, QR), pl.ds(sib_lanes, LANES)],
            W.at[dp, part_rows(0, p)], sib_send.at[p], sib_recv.at[p], (dp, sib),
        )

    row16 = iota((16, LANES), 0)
    lane16 = iota((16, LANES), 1)
    owner = jnp.zeros((16, LANES), jnp.int32)
    spread16 = (lane16 % 16 == row16).astype(F32).astype(BF16)
    slot = dot(page_slot[...].astype(F32).astype(BF16), spread16)
    slot = jnp.where(iota((SESS, LANES), 0) == iota((SESS, LANES), 1) // 16, slot, 0.0)
    slot = jnp.sum(slot, axis=0, keepdims=True).astype(jnp.int32)
    for s in range(SESS):
        here = lane16 == s * 16 + row16
        owner = jnp.where(here, page_owner[s], owner)
    lane = iota((1, LANES), 1)
    owner = jnp.sum(owner.astype(F32), axis=0, keepdims=True).astype(jnp.int32)
    owner = jnp.where(lane < 96, owner, 16)
    count = jnp.zeros((1, LANES), jnp.int32)
    for s in range(SESS):
        count = jnp.where(lane // 16 == s, page_count[s], count)
    stored = (lane % 16 < count).astype(jnp.int32)
    own_hot = (owner == iota((16, LANES), 0)).astype(F32)
    before = (iota((LANES, LANES), 0) < iota((LANES, LANES), 1)).astype(F32).astype(BF16)
    ahead = dot(own_hot.astype(BF16), before)
    rank = jnp.sum(own_hot * ahead, axis=0, keepdims=True).astype(jnp.int32)
    ask_row = jnp.where(stored > 0, owner * 16 + rank, -1)
    got_row = jnp.where(stored > 0, jnp.where(rank < 8, owner * 8 + rank, LANES + owner), -1)
    row_io = iota((256, LANES), 0)
    ask = (ask_row == row_io).astype(F32).astype(BF16)
    slot_hot = (iota((LANES, LANES), 0) == slot).astype(F32).astype(BF16)
    REQ[...] = dot_nt(ask, slot_hot).astype(BF16).reshape(16, 16, LANES)
    RQIN[dp] = REQ[dp]
    for d in range(1, 16):
        to = (dp + d) % 16
        remote(REQ.at[to], RQIN.at[dp], rq_send.at[d], rq_recv.at[d], (to, tn))
    got = (got_row == row_io).astype(F32).T[0:96, :].astype(BF16)

    ld_w.wait()
    advance(1)

    ld_pool.wait()
    pool_low = PL[...].astype(BF16)

    def permute(e, _):
        pick = (iota((PAGE, LANES), 0) - ENT * iota((PAGE, LANES), 1) == e).astype(F32)
        PP[:, pl.ds(pl.multiple_of(e * LANES, LANES), LANES)] = dot(
            pool_low, pick.astype(BF16)
        ).astype(BF16)
        return 0

    lax.fori_loop(0, ENT, permute, 0)
    PP[:, ENT * LANES :] = jnp.zeros((LANES, LANES), BF16)

    for d in range(1, 16):
        src = (dp + 16 - d) % 16
        arrived(RQIN.at[src], rq_send.at[d], rq_recv.at[d])
    asked = RQIN[...].astype(F32)
    first8 = asked[:, 0:8, :].reshape(LANES, LANES).astype(BF16)
    low = dot(first8, PP[:, 0:HALF]).reshape(16, 8, HALF)
    high = dot(first8, PP[:, HALF : 2 * HALF]).reshape(16, 8, HALF)
    PS[...] = jnp.concatenate([low, high], axis=1).astype(BF16)
    ninth = dot(asked[:, 8, :].astype(BF16), PP[...])
    S8[...] = ninth.reshape(16, 1, 2 * HALF)
    PRV[dp] = PS[dp]
    P8[dp] = S8[dp]
    for d in range(1, 16):
        to = (dp + d) % 16
        remote(PS.at[to], PRV.at[dp], pa_send.at[d], pa_recv.at[d], (to, tn))
        remote(S8.at[to], P8.at[dp], pb_send.at[d], pb_recv.at[d], (to, tn))

    advance(4)

    for p in range(CB):
        cols = slice(p * LANES, (p + 1) * LANES)
        SPB[pl.ds(p, KW, stride=CB), :] = conv_w[:, cols]
        SPB[pl.ds(4 * CB + p, 1), :] = conv_b[:, cols]
        SPB[pl.ds(5 * CB + p, 1), :] = skip[:, cols]
        SPB[pl.ds(8 * CB + p, NS, stride=CB), :] = -LOG2E * jnp.exp(decay_log[:, cols])
    CPW[...] = jnp.zeros_like(CPW)
    CPW[0 : 2 * NS, :] = coup_w[...]
    RSS[ROWS:, :] = jnp.zeros((8 * RB - ROWS, PW), BF16)

    ld_x.wait()

    def spread(g, _):
        r = pl.multiple_of(g * 16, 16)
        for p in range(CB):
            S2[pl.ds(g * 256 + p, 16, stride=CB), :] = XN[
                pl.ds(r, 16), p * LANES : (p + 1) * LANES
            ].astype(F32)
        return 0

    lax.fori_loop(0, ROWS // 16, spread, 0)

    taps = [SPB[w * CB : (w + 1) * CB, :] for w in range(KW)]
    bias = SPB[4 * CB : 5 * CB, :]
    none = jnp.zeros((CB, LANES), F32)
    for s in range(SESS):
        raw = [S2[(s * NEW + t) * CB : (s * NEW + t + 1) * CB, :] for t in range(3)]
        for t in range(3):
            pre = bias
            for u in range(t + 1):
                pre = pre + taps[3 - t + u] * raw[u]
            PRE[(s * 3 + t) * CB : (s * 3 + t + 1) * CB, :] = pre

    def conv_session(s, _):
        def step(i, hist):
            h3, h2, h1 = hist
            for u in range(8):
                at = pl.ds(pl.multiple_of((s * NEW + i * 8 + u) * CB, CB), CB)
                now = S2[at, :]
                pre = bias + taps[0] * h3 + taps[1] * h2 + taps[2] * h1 + taps[3] * now
                S2[at, :] = pre * sigmoid(pre)
                h3, h2, h1 = h2, h1, now
            return (h3, h2, h1)

        lax.fori_loop(0, NEW // 8, step, (none, none, none))
        return 0

    lax.fori_loop(0, SESS, conv_session, 0)

    def collect(g, _):
        r = pl.multiple_of(g * 16, 16)
        for p in range(CB):
            XN[pl.ds(r, 16), p * LANES : (p + 1) * LANES] = S2[
                pl.ds(g * 256 + p, 16, stride=CB), :
            ].astype(BF16)
        return 0

    lax.fori_loop(0, ROWS // 16, collect, 0)

    ld_siw.wait()

    def project(m, _):
        r = pl.ds(pl.multiple_of(m * 96, 96), 96)
        RSS[r, 0:RANK] = dot(XN[r, :], SIW[...]).astype(BF16)
        RSS[r, RANK:] = dot_nt(XN[r, :], CPW[...]).astype(BF16)
        return 0

    lax.fori_loop(0, ROWS // 96, project, 0)
    for d in range(1, 8):
        to = (tn + d) % 8
        remote(
            RSS.at[pl.ds(pl.multiple_of(to * RB, 16), RB)], RSR.at[d],
            rs_send.at[d], rs_recv.at[d], (dp, to),
        )
    advance(8)

    EB[...] = (iota((LANES, 2 * NS * LANES), 0) == iota((LANES, 2 * NS * LANES), 1) // LANES).astype(
        F32
    ).astype(BF16)
    advance(8)

    for d in range(1, 16):
        src = (dp + 16 - d) % 16
        arrived(PRV.at[src], pa_send.at[d], pa_recv.at[d])
        arrived(P8.at[src], pb_send.at[d], pb_recv.at[d])

    for s in range(2):
        for o in range(16):
            RALL[o * 8 : o * 8 + 8, :] = PRV[o].astype(F32)[8 * s : 8 * s + 8, :]
        RALL[LANES : LANES + 16, :] = P8[...].reshape(16, 2 * HALF)[:, s * HALF : (s + 1) * HALF]
        RALL[LANES + 16 :, :] = jnp.zeros((LANES - 16, HALF), F32)
        FT[:, s * HALF : (s + 1) * HALF] = dot(got, RALL[...].astype(BF16))


    advance(8)

    F2[SESS * 3 * CB :, :] = jnp.zeros(((FIX - SESS * 3) * CB, LANES), F32)
    for s in range(SESS):
        hist = [
            FT[s * CB : (s + 1) * CB, (NS + w) * LANES : (NS + w + 1) * LANES] for w in range(3)
        ]
        for t in range(3):
            r = s * 3 + t
            pre = PRE[r * CB : (r + 1) * CB, :]
            for w in range(3 - t):
                pre = pre + taps[w] * hist[t + w]
            sg = pre * sigmoid(pre)
            S2[(s * NEW + t) * CB : (s * NEW + t + 1) * CB, :] = sg
            F2[r * CB : (r + 1) * CB, :] = sg
    for p in range(CB):
        XF[:, p * LANES : (p + 1) * LANES] = F2[pl.ds(p, FIX, stride=CB), :].astype(BF16)
    FXS[:, 0:RANK] = dot(XF[...], SIW[...]).astype(BF16)
    FXS[:, RANK:] = dot_nt(XF[...], CPW[...]).astype(BF16)
    for d in range(1, 8):
        to = (tn + d) % 8
        remote(FXS, FXR.at[d], fx_send.at[d], fx_recv.at[d], (dp, to))

    advance(8)

    def normalize(sums):
        low = sums[:, 0:RANK]
        inv_rms = lax.rsqrt(jnp.mean(low * low, axis=-1, keepdims=True) + EPSILON)
        return (low * inv_rms * step_gain[...]).astype(BF16), sums[:, RANK:].astype(BF16)

    mine = pl.ds(pl.multiple_of(tn * RB, 16), RB)
    total = RSS[mine, :].astype(F32)
    for d in range(1, 8):
        arrived(RSR.at[d], rs_send.at[d], rs_recv.at[d])
        total = total + RSR[d].astype(F32)
    AGB[mine, 0:RANK], AGB[mine, RANK:] = normalize(total)
    an_sends = []
    for d in range(1, 8):
        to = (tn + d) % 8
        remote(AGB.at[mine], AGB.at[mine], an_send.at[d], an_recv.at[d], (dp, to), an_sends)
    advance(12)
    for d in range(1, 8):
        src = (tn + 8 - d) % 8
        arrived(
            AGB.at[pl.ds(pl.multiple_of(src * RB, 16), RB)], an_send.at[d], an_recv.at[d]
        )

    fixed = FXS[...].astype(F32)
    for d in range(1, 8):
        arrived(FXR.at[d], fx_send.at[d], fx_recv.at[d])
        fixed = fixed + FXR[d].astype(F32)
    normed, coupled = normalize(fixed)
    place = iota((96, FIX), 0)
    place = ((place % 16 < 3) & (place // 16 * 3 + place % 16 == iota((96, FIX), 1))).astype(F32)
    placed = dot(place.astype(BF16), jnp.concatenate([normed, coupled], axis=1))
    for c in an_sends:
        c.wait_send()
    for s in range(SESS):
        r = slice(s * NEW, s * NEW + 16)
        AGB[r, :] = jnp.where(
            iota((16, PW), 0) < 3, placed[s * 16 : s * 16 + 16, :], AGB[r, :].astype(F32)
        ).astype(BF16)

    advance(16)

    ld_sw.wait()

    def step_size(m, _):
        r = pl.ds(pl.multiple_of(m * 96, 96), 96)
        for p in range(0, CB, 2):
            cols = slice(p * LANES, (p + 2) * LANES)
            v = dot(AGB[r, 0:RANK], SWV[:, cols]) + step_b[:, cols]
            v = jnp.maximum(v, 0.0) + jnp.log1p(jnp.exp(-jnp.abs(v)))
            for i in (0, 1):
                D2[pl.ds(m * 96 * CB + p + i, 96, stride=CB), :] = v[:, i * LANES : (i + 1) * LANES]
        return 0

    lax.fori_loop(0, ROWS // 96, step_size, 0)
    advance(20)

    def gates(first, last):
        for s in range(first, last):
            arrived(G.at[1 - core, pl.ds(s * NEW, NEW)], gx_send.at[s], gx_recv.at[s])

    last_event = {}
    for i, (q, da, db, p) in enumerate(events):
        last_event[(da, db) if q == 0 else (db, da)] = i

    def multiply(pair, halves):
        advance(max(last_event[key] for key in pair) + 1)
        blocks = [((x + 4 - dx) % 4) * 4 + (z + 4 - dz) % 4 for dx, dz in pair]
        r = slice(halves[0] * HROWS, (halves[-1] + 1) * HROWS)

        def weight(k):
            return jnp.concatenate([W[b, k * CH : (k + 1) * CH, :] for b in blocks], axis=1)

        v = dot(G[0, r, :], weight(0)) + dot(G[1, r, :], weight(1))
        for i, b in enumerate(blocks):
            to, side = b // 2, b % 2
            OB[b, r, :] = v[:, i * LANES : (i + 1) * LANES].astype(BF16)

            @pl.when(to != tn)
            def _(b=b, to=to, side=side):
                for g in halves:
                    rg = pl.ds(g * HROWS, HROWS)
                    pltpu.make_async_remote_copy(
                        src_ref=OB.at[b, rg], dst_ref=RBO.at[tn, side, rg],
                        send_sem=ob_send.at[b, g], recv_sem=ob_recv.at[tn, side, g],
                        device_id=(dp, to), device_id_type=MESH,
                    ).start()

            @pl.when(to == tn)
            def _(b=b, side=side, r=r):
                RBO[tn, side, r, :] = OB[b, r, :]

    ld_g.wait()
    outs = []
    for s in range(SESS):
        both = dot(AGB[s * NEW : (s + 1) * NEW, RANK:], EB[...])
        for n in range(2 * NS):
            BC[n * NEW : (n + 1) * NEW, :] = both[:, n * LANES : (n + 1) * LANES]
        for h in (0, 1):
            rate = [SPB[(8 + n) * CB + 8 * h : (8 + n) * CB + 8 * h + 8, :] for n in range(NS)]
            direct = SPB[5 * CB + 8 * h : 5 * CB + 8 * h + 8, :]
            start = tuple(
                FT[s * CB + 8 * h : s * CB + 8 * h + 8, n * LANES : (n + 1) * LANES]
                for n in range(NS)
            )

            def token(i, state, h=h, s=s, rate=rate, direct=direct):
                state = list(state)
                for u in range(4):
                    t = i * 4 + u
                    at = pl.ds(pl.multiple_of((s * NEW + t) * CB + 8 * h, 8), 8)
                    dt, sg = D2[at, :], S2[at, :]
                    dx = dt * sg
                    acc = [direct * sg, None]
                    for n in range(NS):
                        bn = BC[pl.ds(n * NEW + t, 8, stride=0), :]
                        cn = BC[pl.ds((NS + n) * NEW + t, 8, stride=0), :]
                        state[n] = jnp.exp2(dt * rate[n]) * state[n] + dx * bn
                        term = cn * state[n]
                        acc[n % 2] = term if acc[n % 2] is None else acc[n % 2] + term
                    S2[at, :] = acc[0] + acc[1]
                return tuple(state)

            last = lax.fori_loop(0, NEW // 4, token, start)
            advance(20 + (5 * (2 * s + h + 1)) // 3)
            for n in range(NS):
                FSB[n * CB + 8 * h : n * CB + 8 * h + 8, :] = last[n]
        for p in range(CB):
            FSV[s, :, p * LANES : (p + 1) * LANES] = FSB[pl.ds(p, NS, stride=CB), :]
        c = pltpu.make_async_copy(FSV.at[s], final_state.at[s], fs_sem.at[s])
        c.start()
        outs.append(c)

        def gate(g, _, s=s):
            r = pl.ds(pl.multiple_of(s * NEW + g * 16, 16), 16)
            for p in range(CB):
                cols = slice(p * LANES, (p + 1) * LANES)
                gt = GN[r, cols].astype(F32)
                y = S2[pl.ds((s * NEW + g * 16) * CB + p, 16, stride=CB), :]
                G[core, r, cols] = (y * (gt * sigmoid(gt))).astype(BF16)
            return 0

        lax.fori_loop(0, NEW // 16, gate, 0)
        here = G.at[core, pl.ds(s * NEW, NEW)]
        remote(here, here, gx_send.at[s], gx_recv.at[s], (dp, sib))
        if s == SESS // 2 - 1:
            gates(0, s + 1)
            for pair in PAIRS[:EARLY]:
                multiply(pair, (0,))

    gates(SESS // 2, SESS)
    for k, pair in enumerate(PAIRS):
        multiply(pair, (1,) if k < EARLY else (0, 1))
    advance(len(events))

    for side in (1 - z % 2, z % 2):
        for g in (0, 1):
            rg = pl.ds(g * HROWS, HROWS)
            for d in range(1, 8):
                src = (tn + 8 - d) % 8
                arrived(RBO.at[src, side, rg], ob_send.at[0, g], ob_recv.at[src, side, g])
            for c in (0, 1):

                def finish(m, _, c=c, g=g, side=side):
                    r = pl.ds(pl.multiple_of(g * HROWS + m * 96, 32), 96)
                    v = RBO[c, side, r, :].astype(F32)
                    for y in range(1, 4):
                        v = v + RBO[2 * y + c, side, r, :].astype(F32)
                    at = pl.multiple_of(side * 256 + c * LANES, LANES)
                    OUTV[r, pl.ds(at, LANES)] = v.astype(BF16)
                    return 0

                lax.fori_loop(0, HROWS // 96, finish, 0)
            cols = pl.ds(pl.multiple_of(side * 256, 256), 256)
            c = pltpu.make_async_copy(
                OUTV.at[rg, cols], mixer_out.at[rg, cols], out_sem.at[side, g]
            )
            c.start()
            outs.append(c)
    for src in range(16):

        @pl.when(src // 2 != tn)
        def _(src=src):
            for g in (0, 1):
                ref = OB.at[src, pl.ds(g * HROWS, HROWS)]
                pltpu.make_async_remote_copy(
                    src_ref=ref, dst_ref=ref, send_sem=ob_send.at[src, g],
                    recv_sem=ob_recv.at[0, 0, 0], device_id=(dp, tn), device_id_type=MESH,
                ).wait_send()

    for c in sends:
        c.wait_send()
    for c in outs:
        c.wait()


def body(
    conv_input, gate_input, conv_weight, conv_bias, state_pool, page_owner, page_slot, page_count,
    step_in_weight, coupling_weight, step_gain, step_weight, step_bias, decay_log, skip_gain,
    out_weight,
):
    vmem = pl.BlockSpec(memory_space=pltpu.VMEM)
    hbm = pl.BlockSpec(memory_space=pl.ANY)
    sem = pltpu.SemaphoreType.DMA
    mixer_out, final_state = pl.pallas_call(
        kernel,
        out_shape=(
            jax.ShapeDtypeStruct((ROWS, 512), BF16),
            jax.ShapeDtypeStruct((SESS, NS, CH), F32),
        ),
        in_specs=[vmem] * 2 + [pl.BlockSpec(memory_space=pltpu.SMEM)] + [vmem] * 7 + [hbm] * 6,
        out_specs=(hbm, hbm),
        scratch_shapes=[
            pltpu.VMEM((16, 2 * CH, LANES), BF16),
            pltpu.VMEM((2, ROWS, CH), BF16),
            pltpu.VMEM((ROWS, CH), BF16),
            pltpu.VMEM((ROWS, CH), BF16),
            pltpu.VMEM((CH, RANK), BF16),
            pltpu.VMEM((RANK, CH), BF16),
            pltpu.VMEM((ROWS * CB, LANES), F32),
            pltpu.VMEM((ROWS * CB, LANES), F32),
            pltpu.VMEM((LANES, PAGE), F32),
            pltpu.VMEM((LANES, 2 * HALF), BF16),
            pltpu.VMEM((16, 16, LANES), BF16),
            pltpu.VMEM((16, 16, LANES), BF16),
            pltpu.VMEM((16, 16, HALF), BF16),
            pltpu.VMEM((16, 16, HALF), BF16),
            pltpu.VMEM((16, 1, 2 * HALF), F32),
            pltpu.VMEM((16, 1, 2 * HALF), F32),
            pltpu.VMEM((256, HALF), F32),
            pltpu.VMEM((96, 2 * HALF), F32),
            pltpu.VMEM((SESS * 3 * CB, LANES), F32),
            pltpu.VMEM((FIX * CB, LANES), F32),
            pltpu.VMEM((FIX, CH), BF16),
            pltpu.VMEM((FIX, PW), BF16),
            pltpu.VMEM((8, FIX, PW), BF16),
            pltpu.VMEM((24 * CB, LANES), F32),
            pltpu.VMEM((LANES, CH), BF16),
            pltpu.VMEM((8 * RB, PW), BF16),
            pltpu.VMEM((8, RB, PW), BF16),
            pltpu.VMEM((8 * RB, PW), BF16),
            pltpu.VMEM((LANES, 2 * NS * LANES), BF16),
            pltpu.VMEM((2 * NS * NEW, LANES), F32),
            pltpu.VMEM((NS * CB, LANES), F32),
            pltpu.VMEM((SESS, NS, CH), F32),
            pltpu.VMEM((16, ROWS, LANES), BF16),
            pltpu.VMEM((8, 2, ROWS, LANES), BF16),
            pltpu.VMEM((ROWS, 512), BF16),
            sem((6,)), sem((64,)), sem((64,)), sem((2,)), sem((2,)), sem((16,)), sem((16,)),
            sem((16,)), sem((16,)), sem((16,)), sem((16,)), sem((8,)), sem((8,)), sem((8,)), sem((8,)),
            sem((8,)), sem((8,)),
            sem((SESS,)), sem((SESS,)), sem((16, 2)), sem((8, 2, 2)), sem((SESS,)), sem((2, 2)),
        ],
        compiler_params=pltpu.CompilerParams(
            collective_id=0, has_side_effects=True, vmem_limit_bytes=62 << 20
        ),
        cost_estimate=pl.CostEstimate(
            flops=2 * ROWS * CH * (4096 + 1056), bytes_accessed=12 << 20, transcendentals=20 << 20
        ),
    )(
        page_owner, page_slot, page_count,
        conv_weight, conv_bias.reshape(1, -1), coupling_weight, step_gain.reshape(1, -1),
        step_bias.reshape(1, -1), decay_log, skip_gain.reshape(1, -1),
        conv_input.reshape(ROWS, CH), gate_input.reshape(ROWS, CH), state_pool,
        step_in_weight, step_weight, out_weight,
    )
    return mixer_out.reshape(SESS, NEW, 512), final_state


def solution(mesh):
    return jax.shard_map(
        body,
        mesh=mesh,
        in_specs=(
            P("dp", None, "tensor"),
            P("dp", None, "tensor"),
            P(None, "tensor"),
            P("tensor"),
            P("dp", "tensor"),
            P("dp", None, None),
            P("dp", None),
            P("dp"),
            P("tensor", None),
            P(None, "tensor"),
            P(),
            P(None, "tensor"),
            P("tensor"),
            P(None, "tensor"),
            P("tensor"),
            P("tensor", "dp"),
        ),
        out_specs=(P("dp", None, "tensor"), P("dp", None, "tensor")),
        check_vma=False,
    )
```

```python
import jax
import jax.numpy as jnp
from jax import lax
from jax.experimental import pallas as pl
from jax.experimental.pallas import tpu as pltpu
from jax.sharding import PartitionSpec as P

EPSILON = 1e-06
LOG2E = 1.4426950408889634
MESH = pl.DeviceIdType.MESH
F32 = jnp.float32
BF16 = jnp.bfloat16

SESS, NEW, ROWS = 6, 96, 576
CB, LANES, CH = 16, 128, 2048
NS, KW, RANK, ENT = 16, 4, 512, 19
PAGE = CH // CB * ENT
HALF = 10 * LANES
GROUPS = ((0, 4), (4, 6))
GROUP_ROWS = ((0, 48), (384, 32))
PADDED = 640
PW = RANK + LANES
FIX = 32
QR = 1024


def gather_label(q, da, db, p):
    return ((q * 4 + da) * 4 + db) * 2 + p


def gather_events():
    return [
        (0, 0, 0, 0), (0, 0, 0, 1), (1, 0, 0, 0), (1, 0, 0, 1),
        (0, 0, 1, 0), (0, 0, 3, 0), (0, 1, 0, 0), (0, 3, 0, 0),
        (0, 0, 3, 1), (0, 0, 1, 1), (0, 1, 0, 1), (0, 3, 0, 1),
        (1, 1, 0, 0), (1, 0, 3, 0), (1, 0, 1, 0), (1, 3, 0, 0),
        (1, 0, 3, 1), (1, 0, 1, 1), (1, 3, 0, 1), (1, 1, 0, 1),
        (0, 1, 3, 0), (0, 2, 0, 0), (0, 2, 0, 1), (0, 0, 2, 0),
        (0, 1, 1, 0), (0, 3, 3, 0), (1, 1, 3, 0), (1, 1, 1, 0),
        (0, 3, 1, 0), (1, 3, 3, 0), (1, 0, 2, 0), (0, 0, 2, 1),
        (1, 3, 1, 0), (0, 1, 1, 1), (0, 1, 3, 1), (1, 0, 2, 1),
        (1, 3, 1, 1), (1, 3, 3, 1), (0, 3, 1, 1), (0, 3, 3, 1),
        (1, 1, 1, 1), (1, 1, 3, 1), (1, 2, 0, 1), (1, 2, 0, 0),
        (0, 2, 1, 0), (0, 2, 3, 0), (1, 1, 2, 0), (1, 3, 2, 1),
        (0, 2, 1, 1), (0, 2, 3, 1), (1, 3, 2, 0), (1, 1, 2, 1),
        (1, 2, 3, 1), (1, 2, 1, 1), (0, 1, 2, 1), (0, 1, 2, 0),
        (1, 2, 1, 0), (1, 2, 3, 0), (0, 3, 2, 1), (0, 3, 2, 0),
        (0, 2, 2, 0), (0, 2, 2, 1), (1, 2, 2, 1), (1, 2, 2, 0),
    ]


PAIRS = (
    ((0, 0), (0, 1)), ((0, 3), (1, 0)), ((3, 0), (2, 0)), ((1, 3), (3, 3)),
    ((1, 1), (3, 1)), ((0, 2), (2, 1)), ((2, 3), (1, 2)), ((3, 2), (2, 2)),
)
EARLY = 2
HROWS = ROWS // 2


def gather_forwards(q, da, db, p):
    out = []
    if db == 0:
        if da == 0:
            out += [("a", 1, (q, 1, 0, p)), ("a", 3, (q, 3, 0, p))]
        if da == 1 and p == 0:
            out.append(("a", 1, (q, 2, 0, 0)))
        if da == 3 and p == 1:
            out.append(("a", 3, (q, 2, 0, 1)))
        out += [("b", 1, (q, da, 1, p)), ("b", 3, (q, da, 3, p))]
    else:
        if db == 1 and p == 0:
            out.append(("b", 1, (q, da, 2, 0)))
        if db == 3 and p == 1:
            out.append(("b", 3, (q, da, 2, 1)))
    return out


def sigmoid(v):
    return 0.5 * (1.0 + jnp.tanh(0.5 * v))


def dot_nt(a, b):
    return lax.dot_general(a, b, (((1,), (1,)), ((), ())), preferred_element_type=F32)


def dot(a, b):
    return jnp.dot(a, b, preferred_element_type=F32)


def iota(shape, dim):
    return lax.broadcasted_iota(jnp.int32, shape, dim)


def kernel(
    page_owner, page_slot, page_count, conv_w, conv_b, coup_w, step_gain, step_b, decay_log, skip,
    conv_in, gate_in, pool, step_in_w, step_w, out_w,
    mixer_out, final_state,
    W, G, XN, GN, SIW, SWV, S2, D2, PL, PP, REQ, RQIN, PS, PRV, S8, P8, RALL, FT,
    PRE, F2, XF, FXS, FXR,
    SPB, CPW, RSS, RSR, AGB, FXP, EB, BC, FSB, FSV, OB, RBO, OUTV,
    loc_sem, ag_send, ag_recv, sib_send, sib_recv, rq_send, rq_recv,
    pa_send, pa_recv, pb_send, pb_recv, rs_send, rs_recv, an_send, an_recv, fx_send, fx_recv,
    gx_send, gx_recv, ob_send, ob_recv, fs_sem, out_sem,
):
    dp = lax.axis_index("dp")
    tn = lax.axis_index("tensor")
    x, z = dp // 4, dp % 4
    core = tn % 2
    sib = tn + 1 - 2 * core
    sends = []

    def remote(src, dst, ssem, rsem, to, kept=sends):
        c = pltpu.make_async_remote_copy(
            src_ref=src, dst_ref=dst, send_sem=ssem, recv_sem=rsem,
            device_id=to, device_id_type=MESH,
        )
        c.start()
        kept.append(c)

    def arrived(ref, ssem, rsem):
        pltpu.make_async_remote_copy(
            src_ref=ref, dst_ref=ref, send_sem=ssem, recv_sem=rsem,
            device_id=(dp, tn), device_id_type=MESH,
        ).wait_recv()

    def local(src, dst, k):
        c = pltpu.make_async_copy(src, dst, loc_sem.at[k])
        c.start()
        return c

    own_rows = pl.multiple_of(core * CH, CH)
    sib_rows = pl.multiple_of(CH - core * CH, CH)
    own_lanes = pl.multiple_of(core * LANES, LANES)
    sib_lanes = pl.multiple_of(LANES - core * LANES, LANES)
    ld_w = local(out_w.at[:, pl.ds(own_lanes, LANES)], W.at[dp, pl.ds(own_rows, CH)], 0)
    ld_pool = local(pool, PL, 1)
    ld_x = local(conv_in, XN, 2)
    ld_siw = local(step_in_w, SIW, 3)
    ld_sw = local(step_w, SWV, 4)
    ld_g = local(gate_in, GN, 5)

    bar = pltpu.get_barrier_semaphore()
    for d in range(1, 16):
        pl.semaphore_signal(bar, inc=1, device_id=((dp + d) % 16, tn), device_id_type=MESH)
    for d in range(1, 8):
        pl.semaphore_signal(bar, inc=1, device_id=(dp, (tn + d) % 8), device_id_type=MESH)
    pl.semaphore_wait(bar, 22)

    def part_rows(q, p):
        base = own_rows if q == 0 else sib_rows
        return pl.ds(pl.multiple_of(base + p * QR, QR), QR)

    def dp_of(q, a, b):
        return a * 4 + b if q == 0 else b * 4 + a

    def coords(q):
        return (x, z) if q == 0 else (z, x)

    def part(q, da, db, p):
        a, b = coords(q)
        return W.at[dp_of(q, (a + 4 - da) % 4, (b + 4 - db) % 4), part_rows(q, p)]

    def gather_step(label):
        q, da, db, p = label
        a, b = coords(q)
        ref = part(q, da, db, p)
        if (da, db) != (0, 0):
            k = gather_label(*label)
            arrived(ref, ag_send.at[k], ag_recv.at[k])
        elif q == 1:
            arrived(ref, sib_send.at[p], sib_recv.at[p])
        for axis, step, nlabel in gather_forwards(*label):
            k = gather_label(*nlabel)
            to = ((a + step) % 4, b) if axis == "a" else (a, (b + step) % 4)
            remote(ref, ref, ag_send.at[k], ag_recv.at[k], (dp_of(q, *to), tn))

    events = gather_events()
    cursor = [0]

    def advance(upto):
        while cursor[0] < min(upto, len(events)):
            gather_step(events[cursor[0]])
            cursor[0] += 1

    for p in (0, 1):
        remote(
            out_w.at[pl.ds(p * QR, QR), pl.ds(sib_lanes, LANES)],
            W.at[dp, part_rows(0, p)], sib_send.at[p], sib_recv.at[p], (dp, sib),
        )

    row16 = iota((16, LANES), 0)
    lane16 = iota((16, LANES), 1)
    owner = jnp.zeros((16, LANES), jnp.int32)
    spread16 = (lane16 % 16 == row16).astype(F32).astype(BF16)
    slot = dot(page_slot[...].astype(F32).astype(BF16), spread16)
    slot = jnp.where(iota((SESS, LANES), 0) == iota((SESS, LANES), 1) // 16, slot, 0.0)
    slot = jnp.sum(slot, axis=0, keepdims=True).astype(jnp.int32)
    for s in range(SESS):
        here = lane16 == s * 16 + row16
        owner = jnp.where(here, page_owner[s], owner)
    lane = iota((1, LANES), 1)
    owner = jnp.sum(owner.astype(F32), axis=0, keepdims=True).astype(jnp.int32)
    owner = jnp.where(lane < 96, owner, 16)
    count = jnp.zeros((1, LANES), jnp.int32)
    for s in range(SESS):
        count = jnp.where(lane // 16 == s, page_count[s], count)
    stored = (lane % 16 < count).astype(jnp.int32)
    own_hot = (owner == iota((16, LANES), 0)).astype(F32)
    before = (iota((LANES, LANES), 0) < iota((LANES, LANES), 1)).astype(F32).astype(BF16)
    ahead = dot(own_hot.astype(BF16), before)
    rank = jnp.sum(own_hot * ahead, axis=0, keepdims=True).astype(jnp.int32)
    ask_row = jnp.where(stored > 0, owner * 16 + rank, -1)
    got_row = jnp.where(stored > 0, jnp.where(rank < 8, owner * 8 + rank, LANES + owner), -1)
    row_io = iota((256, LANES), 0)
    ask = (ask_row == row_io).astype(F32).astype(BF16)
    slot_hot = (iota((LANES, LANES), 0) == slot).astype(F32).astype(BF16)
    REQ[...] = dot_nt(ask, slot_hot).astype(BF16).reshape(16, 16, LANES)
    RQIN[dp] = REQ[dp]
    for d in range(1, 16):
        to = (dp + d) % 16
        remote(REQ.at[to], RQIN.at[dp], rq_send.at[d], rq_recv.at[d], (to, tn))
    got = (got_row == row_io).astype(F32).T[0:96, :].astype(BF16)

    ld_w.wait()
    advance(1)

    ld_pool.wait()
    pool_low = PL[...].astype(BF16)

    def permute(e, _):
        pick = (iota((PAGE, LANES), 0) - ENT * iota((PAGE, LANES), 1) == e).astype(F32)
        PP[:, pl.ds(pl.multiple_of(e * LANES, LANES), LANES)] = dot(
            pool_low, pick.astype(BF16)
        ).astype(BF16)
        return 0

    lax.fori_loop(0, ENT, permute, 0)
    PP[:, ENT * LANES :] = jnp.zeros((LANES, LANES), BF16)

    for d in range(1, 16):
        src = (dp + 16 - d) % 16
        arrived(RQIN.at[src], rq_send.at[d], rq_recv.at[d])
    asked = RQIN[...].astype(F32)
    first8 = asked[:, 0:8, :].reshape(LANES, LANES).astype(BF16)
    low = dot(first8, PP[:, 0:HALF]).reshape(16, 8, HALF)
    high = dot(first8, PP[:, HALF : 2 * HALF]).reshape(16, 8, HALF)
    PS[...] = jnp.concatenate([low, high], axis=1).astype(BF16)
    ninth = dot(asked[:, 8, :].astype(BF16), PP[...])
    S8[...] = ninth.reshape(16, 1, 2 * HALF)
    PRV[dp] = PS[dp]
    P8[dp] = S8[dp]
    for d in range(1, 16):
        to = (dp + d) % 16
        remote(PS.at[to], PRV.at[dp], pa_send.at[d], pa_recv.at[d], (to, tn))
        remote(S8.at[to], P8.at[dp], pb_send.at[d], pb_recv.at[d], (to, tn))

    advance(4)

    for p in range(CB):
        cols = slice(p * LANES, (p + 1) * LANES)
        SPB[pl.ds(p, KW, stride=CB), :] = conv_w[:, cols]
        SPB[pl.ds(4 * CB + p, 1), :] = conv_b[:, cols]
        SPB[pl.ds(5 * CB + p, 1), :] = skip[:, cols]
        SPB[pl.ds(8 * CB + p, NS, stride=CB), :] = -LOG2E * jnp.exp(decay_log[:, cols])
    CPW[...] = jnp.zeros_like(CPW)
    CPW[0 : 2 * NS, :] = coup_w[...]
    RSS[ROWS:, :] = jnp.zeros((PADDED - ROWS, PW), BF16)

    ld_x.wait()

    def spread(g, _):
        r = pl.multiple_of(g * 16, 16)
        for p in range(CB):
            S2[pl.ds(g * 256 + p, 16, stride=CB), :] = XN[
                pl.ds(r, 16), p * LANES : (p + 1) * LANES
            ].astype(F32)
        return 0

    lax.fori_loop(0, ROWS // 16, spread, 0)

    taps = [SPB[w * CB : (w + 1) * CB, :] for w in range(KW)]
    bias = SPB[4 * CB : 5 * CB, :]
    none = jnp.zeros((CB, LANES), F32)
    for s in range(SESS):
        raw = [S2[(s * NEW + t) * CB : (s * NEW + t + 1) * CB, :] for t in range(3)]
        for t in range(3):
            pre = bias
            for u in range(t + 1):
                pre = pre + taps[3 - t + u] * raw[u]
            PRE[(s * 3 + t) * CB : (s * 3 + t + 1) * CB, :] = pre

    def conv_session(s, _):
        def step(i, hist):
            h3, h2, h1 = hist
            for u in range(8):
                at = pl.ds(pl.multiple_of((s * NEW + i * 8 + u) * CB, CB), CB)
                now = S2[at, :]
                pre = bias + taps[0] * h3 + taps[1] * h2 + taps[2] * h1 + taps[3] * now
                S2[at, :] = pre * sigmoid(pre)
                h3, h2, h1 = h2, h1, now
            return (h3, h2, h1)

        lax.fori_loop(0, NEW // 8, step, (none, none, none))
        return 0

    def collect(g, _):
        r = pl.multiple_of(g * 16, 16)
        for p in range(CB):
            XN[pl.ds(r, 16), p * LANES : (p + 1) * LANES] = S2[
                pl.ds(g * 256 + p, 16, stride=CB), :
            ].astype(BF16)
        return 0

    ld_siw.wait()

    def project(m, _):
        r = pl.ds(pl.multiple_of(m * 96, 96), 96)
        RSS[r, 0:RANK] = dot(XN[r, :], SIW[...]).astype(BF16)
        RSS[r, RANK:] = dot_nt(XN[r, :], CPW[...]).astype(BF16)
        return 0

    def prepare(group):
        first, last = GROUPS[group]
        lax.fori_loop(first, last, conv_session, 0)
        lax.fori_loop(first * NEW // 16, last * NEW // 16, collect, 0)
        lax.fori_loop(first, last, project, 0)

    def share(group, who):
        base, rows = GROUP_ROWS[group]
        return pl.ds(pl.multiple_of(base + who * rows, 16), rows)

    def landing(group):
        return pl.ds(48 * group, GROUP_ROWS[group][1])

    def send_sums(group):
        for d in range(1, 8):
            to = (tn + d) % 8
            remote(
                RSS.at[share(group, to)], RSR.at[d, landing(group)],
                rs_send.at[group, d], rs_recv.at[group, d], (dp, to),
            )

    prepare(0)
    send_sums(0)
    advance(8)
    prepare(1)

    EB[...] = (iota((LANES, 2 * NS * LANES), 0) == iota((LANES, 2 * NS * LANES), 1) // LANES).astype(
        F32
    ).astype(BF16)
    advance(8)

    for d in range(1, 16):
        src = (dp + 16 - d) % 16
        arrived(PRV.at[src], pa_send.at[d], pa_recv.at[d])
        arrived(P8.at[src], pb_send.at[d], pb_recv.at[d])

    for s in range(2):
        for o in range(16):
            RALL[o * 8 : o * 8 + 8, :] = PRV[o].astype(F32)[8 * s : 8 * s + 8, :]
        RALL[LANES : LANES + 16, :] = P8[...].reshape(16, 2 * HALF)[:, s * HALF : (s + 1) * HALF]
        RALL[LANES + 16 :, :] = jnp.zeros((LANES - 16, HALF), F32)
        FT[:, s * HALF : (s + 1) * HALF] = dot(got, RALL[...].astype(BF16))


    advance(8)

    F2[SESS * 3 * CB :, :] = jnp.zeros(((FIX - SESS * 3) * CB, LANES), F32)
    for s in range(SESS):
        hist = [
            FT[s * CB : (s + 1) * CB, (NS + w) * LANES : (NS + w + 1) * LANES] for w in range(3)
        ]
        for t in range(3):
            r = s * 3 + t
            pre = PRE[r * CB : (r + 1) * CB, :]
            for w in range(3 - t):
                pre = pre + taps[w] * hist[t + w]
            sg = pre * sigmoid(pre)
            S2[(s * NEW + t) * CB : (s * NEW + t + 1) * CB, :] = sg
            F2[r * CB : (r + 1) * CB, :] = sg
    for p in range(CB):
        XF[:, p * LANES : (p + 1) * LANES] = F2[pl.ds(p, FIX, stride=CB), :].astype(BF16)
    FXS[:, 0:RANK] = dot(XF[...], SIW[...]).astype(BF16)
    FXS[:, RANK:] = dot_nt(XF[...], CPW[...]).astype(BF16)
    for d in range(1, 8):
        to = (tn + d) % 8
        remote(FXS, FXR.at[d], fx_send.at[d], fx_recv.at[d], (dp, to))

    advance(8)

    def normalize(sums):
        low = sums[:, 0:RANK]
        inv_rms = lax.rsqrt(jnp.mean(low * low, axis=-1, keepdims=True) + EPSILON)
        return (low * inv_rms * step_gain[...]).astype(BF16), sums[:, RANK:].astype(BF16)

    an_sends = ([], [])

    def spread_normed(group):
        mine = share(group, tn)
        total = RSS[mine, :].astype(F32)
        for d in range(1, 8):
            ref = RSR.at[d, landing(group)]
            arrived(ref, rs_send.at[group, d], rs_recv.at[group, d])
            total = total + ref[...].astype(F32)
        AGB[mine, 0:RANK], AGB[mine, RANK:] = normalize(total)
        for d in range(1, 8):
            to = (tn + d) % 8
            remote(
                AGB.at[mine], AGB.at[mine], an_send.at[group, d], an_recv.at[group, d],
                (dp, to), an_sends[group],
            )

    def take_normed(group):
        for d in range(1, 8):
            src = (tn + 8 - d) % 8
            arrived(AGB.at[share(group, src)], an_send.at[group, d], an_recv.at[group, d])
        for c in an_sends[group]:
            c.wait_send()

    spread_normed(0)
    send_sums(1)
    advance(12)
    take_normed(0)

    fixed = FXS[...].astype(F32)
    for d in range(1, 8):
        arrived(FXR.at[d], fx_send.at[d], fx_recv.at[d])
        fixed = fixed + FXR[d].astype(F32)
    normed, coupled = normalize(fixed)
    place = iota((96, FIX), 0)
    place = ((place % 16 < 3) & (place // 16 * 3 + place % 16 == iota((96, FIX), 1))).astype(F32)
    FXP[...] = dot(place.astype(BF16), jnp.concatenate([normed, coupled], axis=1))

    def correct(group):
        for s in range(*GROUPS[group]):
            r = slice(s * NEW, s * NEW + 16)
            AGB[r, :] = jnp.where(
                iota((16, PW), 0) < 3, FXP[s * 16 : s * 16 + 16, :], AGB[r, :].astype(F32)
            ).astype(BF16)

    correct(0)
    advance(16)

    ld_sw.wait()

    def step_size(m, _):
        r = pl.ds(pl.multiple_of(m * 96, 96), 96)
        for p in range(0, CB, 2):
            cols = slice(p * LANES, (p + 2) * LANES)
            v = dot(AGB[r, 0:RANK], SWV[:, cols]) + step_b[:, cols]
            v = jnp.maximum(v, 0.0) + jnp.log1p(jnp.exp(-jnp.abs(v)))
            for i in (0, 1):
                D2[pl.ds(m * 96 * CB + p + i, 96, stride=CB), :] = v[:, i * LANES : (i + 1) * LANES]
        return 0

    lax.fori_loop(*GROUPS[0], step_size, 0)
    advance(18)

    def gates(first, last):
        for s in range(first, last):
            arrived(G.at[1 - core, pl.ds(s * NEW, NEW)], gx_send.at[s], gx_recv.at[s])

    last_event = {}
    for i, (q, da, db, p) in enumerate(events):
        last_event[(da, db) if q == 0 else (db, da)] = i

    def multiply(pair, halves):
        advance(max(last_event[key] for key in pair) + 1)
        blocks = [((x + 4 - dx) % 4) * 4 + (z + 4 - dz) % 4 for dx, dz in pair]
        r = slice(halves[0] * HROWS, (halves[-1] + 1) * HROWS)

        def weight(k):
            return jnp.concatenate([W[b, k * CH : (k + 1) * CH, :] for b in blocks], axis=1)

        v = dot(G[0, r, :], weight(0)) + dot(G[1, r, :], weight(1))
        for i, b in enumerate(blocks):
            to, side = b // 2, b % 2
            OB[b, r, :] = v[:, i * LANES : (i + 1) * LANES].astype(BF16)

            @pl.when(to != tn)
            def _(b=b, to=to, side=side):
                for g in halves:
                    rg = pl.ds(g * HROWS, HROWS)
                    pltpu.make_async_remote_copy(
                        src_ref=OB.at[b, rg], dst_ref=RBO.at[tn, side, rg],
                        send_sem=ob_send.at[b, g], recv_sem=ob_recv.at[tn, side, g],
                        device_id=(dp, to), device_id_type=MESH,
                    ).start()

            @pl.when(to == tn)
            def _(b=b, side=side, r=r):
                RBO[tn, side, r, :] = OB[b, r, :]

    ld_g.wait()
    outs = []
    for s in range(SESS):
        if s == 1:
            spread_normed(1)
        if s == GROUPS[1][0]:
            take_normed(1)
            correct(1)
            lax.fori_loop(*GROUPS[1], step_size, 0)
        both = dot(AGB[s * NEW : (s + 1) * NEW, RANK:], EB[...])
        for n in range(2 * NS):
            BC[n * NEW : (n + 1) * NEW, :] = both[:, n * LANES : (n + 1) * LANES]
        for h in (0, 1):
            rate = [SPB[(8 + n) * CB + 8 * h : (8 + n) * CB + 8 * h + 8, :] for n in range(NS)]
            direct = SPB[5 * CB + 8 * h : 5 * CB + 8 * h + 8, :]
            start = tuple(
                FT[s * CB + 8 * h : s * CB + 8 * h + 8, n * LANES : (n + 1) * LANES]
                for n in range(NS)
            )

            def token(i, state, h=h, s=s, rate=rate, direct=direct):
                state = list(state)
                for u in range(4):
                    t = i * 4 + u
                    at = pl.ds(pl.multiple_of((s * NEW + t) * CB + 8 * h, 8), 8)
                    dt, sg = D2[at, :], S2[at, :]
                    dx = dt * sg
                    acc = [direct * sg, None]
                    for n in range(NS):
                        bn = BC[pl.ds(n * NEW + t, 8, stride=0), :]
                        cn = BC[pl.ds((NS + n) * NEW + t, 8, stride=0), :]
                        state[n] = jnp.exp2(dt * rate[n]) * state[n] + dx * bn
                        term = cn * state[n]
                        acc[n % 2] = term if acc[n % 2] is None else acc[n % 2] + term
                    S2[at, :] = acc[0] + acc[1]
                return tuple(state)

            last = lax.fori_loop(0, NEW // 4, token, start)
            advance(18 + (26 * (2 * s + h + 1)) // 12)
            for n in range(NS):
                FSB[n * CB + 8 * h : n * CB + 8 * h + 8, :] = last[n]
        for p in range(CB):
            FSV[s, :, p * LANES : (p + 1) * LANES] = FSB[pl.ds(p, NS, stride=CB), :]
        c = pltpu.make_async_copy(FSV.at[s], final_state.at[s], fs_sem.at[s])
        c.start()
        outs.append(c)

        def gate(g, _, s=s):
            r = pl.ds(pl.multiple_of(s * NEW + g * 16, 16), 16)
            for p in range(CB):
                cols = slice(p * LANES, (p + 1) * LANES)
                gt = GN[r, cols].astype(F32)
                y = S2[pl.ds((s * NEW + g * 16) * CB + p, 16, stride=CB), :]
                G[core, r, cols] = (y * (gt * sigmoid(gt))).astype(BF16)
            return 0

        lax.fori_loop(0, NEW // 16, gate, 0)
        here = G.at[core, pl.ds(s * NEW, NEW)]
        remote(here, here, gx_send.at[s], gx_recv.at[s], (dp, sib))
        if s == SESS // 2 - 1:
            gates(0, s + 1)
            for pair in PAIRS[:EARLY]:
                multiply(pair, (0,))

    advance(48)
    gates(SESS // 2, SESS)
    for k, pair in enumerate(PAIRS):
        multiply(pair, (1,) if k < EARLY else (0, 1))
    advance(len(events))

    for side in (1 - z % 2, z % 2):
        for g in (0, 1):
            rg = pl.ds(g * HROWS, HROWS)
            for d in range(1, 8):
                src = (tn + 8 - d) % 8
                arrived(RBO.at[src, side, rg], ob_send.at[0, g], ob_recv.at[src, side, g])
            for c in (0, 1):

                def finish(m, _, c=c, g=g, side=side):
                    r = pl.ds(pl.multiple_of(g * HROWS + m * 96, 32), 96)
                    v = RBO[c, side, r, :].astype(F32)
                    for y in range(1, 4):
                        v = v + RBO[2 * y + c, side, r, :].astype(F32)
                    at = pl.multiple_of(side * 256 + c * LANES, LANES)
                    OUTV[r, pl.ds(at, LANES)] = v.astype(BF16)
                    return 0

                lax.fori_loop(0, HROWS // 96, finish, 0)
            cols = pl.ds(pl.multiple_of(side * 256, 256), 256)
            c = pltpu.make_async_copy(
                OUTV.at[rg, cols], mixer_out.at[rg, cols], out_sem.at[side, g]
            )
            c.start()
            outs.append(c)
    for src in range(16):

        @pl.when(src // 2 != tn)
        def _(src=src):
            for g in (0, 1):
                ref = OB.at[src, pl.ds(g * HROWS, HROWS)]
                pltpu.make_async_remote_copy(
                    src_ref=ref, dst_ref=ref, send_sem=ob_send.at[src, g],
                    recv_sem=ob_recv.at[0, 0, 0], device_id=(dp, tn), device_id_type=MESH,
                ).wait_send()

    for c in sends:
        c.wait_send()
    for c in outs:
        c.wait()


def settle(mixer_in, state_in, mixer_out, state_out, mixer, state, sems):
    hops = []
    for i, (src, via, dst) in enumerate(
        ((state_in, state, state_out), (mixer_in, mixer, mixer_out))
    ):
        for s in range(0, SESS, 2):
            part = pl.ds(s, 2)
            first = pltpu.make_async_copy(src.at[part], via.at[part], sems.at[0, i, s])
            last = pltpu.make_async_copy(via.at[part], dst.at[part], sems.at[1, i, s])
            first.start()
            hops.append((first, last))
    for first, last in hops:
        first.wait()
        last.start()
    for first, last in hops:
        last.wait()


def body(
    conv_input, gate_input, conv_weight, conv_bias, state_pool, page_owner, page_slot, page_count,
    step_in_weight, coupling_weight, step_gain, step_weight, step_bias, decay_log, skip_gain,
    out_weight,
):
    vmem = pl.BlockSpec(memory_space=pltpu.VMEM)
    hbm = pl.BlockSpec(memory_space=pl.ANY)
    sem = pltpu.SemaphoreType.DMA
    mixer_out, final_state = pl.pallas_call(
        kernel,
        out_shape=(
            jax.ShapeDtypeStruct((ROWS, 512), BF16),
            jax.ShapeDtypeStruct((SESS, NS, CH), F32),
        ),
        in_specs=[vmem] * 2 + [pl.BlockSpec(memory_space=pltpu.SMEM)] + [vmem] * 7 + [hbm] * 6,
        out_specs=(hbm, hbm),
        scratch_shapes=[
            pltpu.VMEM((16, 2 * CH, LANES), BF16),
            pltpu.VMEM((2, ROWS, CH), BF16),
            pltpu.VMEM((ROWS, CH), BF16),
            pltpu.VMEM((ROWS, CH), BF16),
            pltpu.VMEM((CH, RANK), BF16),
            pltpu.VMEM((RANK, CH), BF16),
            pltpu.VMEM((ROWS * CB, LANES), F32),
            pltpu.VMEM((ROWS * CB, LANES), F32),
            pltpu.VMEM((LANES, PAGE), F32),
            pltpu.VMEM((LANES, 2 * HALF), BF16),
            pltpu.VMEM((16, 16, LANES), BF16),
            pltpu.VMEM((16, 16, LANES), BF16),
            pltpu.VMEM((16, 16, HALF), BF16),
            pltpu.VMEM((16, 16, HALF), BF16),
            pltpu.VMEM((16, 1, 2 * HALF), F32),
            pltpu.VMEM((16, 1, 2 * HALF), F32),
            pltpu.VMEM((256, HALF), F32),
            pltpu.VMEM((96, 2 * HALF), F32),
            pltpu.VMEM((SESS * 3 * CB, LANES), F32),
            pltpu.VMEM((FIX * CB, LANES), F32),
            pltpu.VMEM((FIX, CH), BF16),
            pltpu.VMEM((FIX, PW), BF16),
            pltpu.VMEM((8, FIX, PW), BF16),
            pltpu.VMEM((24 * CB, LANES), F32),
            pltpu.VMEM((LANES, CH), BF16),
            pltpu.VMEM((PADDED, PW), BF16),
            pltpu.VMEM((8, 80, PW), BF16),
            pltpu.VMEM((PADDED, PW), BF16),
            pltpu.VMEM((96, PW), F32),
            pltpu.VMEM((LANES, 2 * NS * LANES), BF16),
            pltpu.VMEM((2 * NS * NEW, LANES), F32),
            pltpu.VMEM((NS * CB, LANES), F32),
            pltpu.VMEM((SESS, NS, CH), F32),
            pltpu.VMEM((16, ROWS, LANES), BF16),
            pltpu.VMEM((8, 2, ROWS, LANES), BF16),
            pltpu.VMEM((ROWS, 512), BF16),
            sem((6,)), sem((64,)), sem((64,)), sem((2,)), sem((2,)), sem((16,)), sem((16,)),
            sem((16,)), sem((16,)), sem((16,)), sem((16,)), sem((2, 8)), sem((2, 8)),
            sem((2, 8)), sem((2, 8)), sem((8,)), sem((8,)),
            sem((SESS,)), sem((SESS,)), sem((16, 2)), sem((8, 2, 2)), sem((SESS,)), sem((2, 2)),
        ],
        compiler_params=pltpu.CompilerParams(
            collective_id=0, has_side_effects=True, vmem_limit_bytes=62 << 20
        ),
        cost_estimate=pl.CostEstimate(
            flops=2 * ROWS * CH * (4096 + 1056), bytes_accessed=12 << 20, transcendentals=20 << 20
        ),
    )(
        page_owner, page_slot, page_count,
        conv_weight, conv_bias.reshape(1, -1), coupling_weight, step_gain.reshape(1, -1),
        step_bias.reshape(1, -1), decay_log, skip_gain.reshape(1, -1),
        conv_input.reshape(ROWS, CH), gate_input.reshape(ROWS, CH), state_pool,
        step_in_weight, step_weight, out_weight,
    )
    mixer_out = mixer_out.reshape(SESS, NEW, 512)
    return pl.pallas_call(
        settle,
        out_shape=(
            jax.ShapeDtypeStruct(mixer_out.shape, BF16),
            jax.ShapeDtypeStruct(final_state.shape, F32),
        ),
        in_specs=[hbm, hbm],
        out_specs=(hbm, hbm),
        scratch_shapes=[
            pltpu.VMEM(mixer_out.shape, BF16), pltpu.VMEM(final_state.shape, F32), sem((2, 2, SESS)),
        ],
    )(mixer_out, final_state)


def solution(mesh):
    return jax.shard_map(
        body,
        mesh=mesh,
        in_specs=(
            P("dp", None, "tensor"),
            P("dp", None, "tensor"),
            P(None, "tensor"),
            P("tensor"),
            P("dp", "tensor"),
            P("dp", None, None),
            P("dp", None),
            P("dp"),
            P("tensor", None),
            P(None, "tensor"),
            P(),
            P(None, "tensor"),
            P("tensor"),
            P(None, "tensor"),
            P("tensor"),
            P("tensor", "dp"),
        ),
        out_specs=(P("dp", None, "tensor"), P("dp", None, "tensor")),
        check_vma=False,
    )
```

```python
import jax
import jax.numpy as jnp
from jax import lax
from jax.experimental import pallas as pl
from jax.experimental.pallas import tpu as pltpu
from jax.sharding import PartitionSpec as P

EPSILON = 1e-06
LOG2E = 1.4426950408889634
MESH = pl.DeviceIdType.MESH
F32 = jnp.float32
BF16 = jnp.bfloat16

SESS, NEW, ROWS = 6, 96, 576
CB, LANES, CH = 16, 128, 2048
NS, KW, RANK, ENT = 16, 4, 512, 19
PAGE = CH // CB * ENT
HALF = 10 * LANES
GROUPS = ((0, 4), (4, 6))
GROUP_ROWS = ((0, 48), (384, 32))
PADDED = 640
PW = RANK + LANES
FIX = 32
QR = 1024


def gather_label(q, da, db, p):
    return ((q * 4 + da) * 4 + db) * 2 + p


def gather_events():
    return [
        (0, 0, 0, 0), (0, 0, 0, 1), (1, 0, 0, 0), (1, 0, 0, 1),
        (0, 0, 1, 0), (0, 0, 3, 0), (0, 1, 0, 0), (0, 3, 0, 0),
        (0, 0, 3, 1), (0, 0, 1, 1), (0, 1, 0, 1), (0, 3, 0, 1),
        (1, 1, 0, 0), (1, 0, 3, 0), (1, 0, 1, 0), (1, 3, 0, 0),
        (1, 0, 3, 1), (1, 0, 1, 1), (1, 3, 0, 1), (1, 1, 0, 1),
        (0, 1, 3, 0), (0, 2, 0, 0), (0, 2, 0, 1), (0, 0, 2, 0),
        (0, 1, 1, 0), (0, 3, 3, 0), (1, 1, 3, 0), (1, 1, 1, 0),
        (0, 3, 1, 0), (1, 3, 3, 0), (1, 0, 2, 0), (0, 0, 2, 1),
        (1, 3, 1, 0), (0, 1, 1, 1), (0, 1, 3, 1), (1, 0, 2, 1),
        (1, 3, 1, 1), (1, 3, 3, 1), (0, 3, 1, 1), (0, 3, 3, 1),
        (1, 1, 1, 1), (1, 1, 3, 1), (1, 2, 0, 1), (1, 2, 0, 0),
        (0, 2, 1, 0), (0, 2, 3, 0), (1, 1, 2, 0), (1, 3, 2, 1),
        (0, 2, 1, 1), (0, 2, 3, 1), (1, 3, 2, 0), (1, 1, 2, 1),
        (1, 2, 3, 1), (1, 2, 1, 1), (0, 1, 2, 1), (0, 1, 2, 0),
        (1, 2, 1, 0), (1, 2, 3, 0), (0, 3, 2, 1), (0, 3, 2, 0),
        (0, 2, 2, 0), (0, 2, 2, 1), (1, 2, 2, 1), (1, 2, 2, 0),
    ]


PAIRS = (
    ((0, 0), (0, 1)), ((0, 3), (1, 0)), ((3, 0), (2, 0)), ((1, 3), (3, 3)),
    ((1, 1), (3, 1)), ((0, 2), (2, 1)), ((2, 3), (1, 2)), ((3, 2),), ((2, 2),),
)
EARLY = {2: (0, 2), 4: (2, 4)}
SOON = 4
HROWS = ROWS // 2


def gather_forwards(q, da, db, p):
    out = []
    if db == 0:
        if da == 0:
            out += [("a", 1, (q, 1, 0, p)), ("a", 3, (q, 3, 0, p))]
        if da == 1 and p == 0:
            out.append(("a", 1, (q, 2, 0, 0)))
        if da == 3 and p == 1:
            out.append(("a", 3, (q, 2, 0, 1)))
        out += [("b", 1, (q, da, 1, p)), ("b", 3, (q, da, 3, p))]
    else:
        if db == 1 and p == 0:
            out.append(("b", 1, (q, da, 2, 0)))
        if db == 3 and p == 1:
            out.append(("b", 3, (q, da, 2, 1)))
    return out


def sigmoid(v):
    return 0.5 * (1.0 + jnp.tanh(0.5 * v))


def dot_nt(a, b):
    return lax.dot_general(a, b, (((1,), (1,)), ((), ())), preferred_element_type=F32)


def dot(a, b):
    return jnp.dot(a, b, preferred_element_type=F32)


def iota(shape, dim):
    return lax.broadcasted_iota(jnp.int32, shape, dim)


def kernel(
    page_owner, page_slot, page_count, conv_w, conv_b, coup_w, step_gain, step_b, decay_log, skip,
    conv_in, gate_in, pool, step_in_w, step_w, out_w,
    mixer_out, final_state,
    W, G, XN, GN, SIW, SWV, S2, D2, PL, PP, REQ, RQIN, PS, PRV, S8, P8, RALL, FT,
    PRE, F2, XF, FXS, FXR,
    SPB, CPW, RSS, RSR, AGB, FXP, EB, BC, FSB, FSV, OB, RBO, OUTV,
    loc_sem, ag_send, ag_recv, sib_send, sib_recv, rq_send, rq_recv,
    pa_send, pa_recv, pb_send, pb_recv, rs_send, rs_recv, an_send, an_recv, fx_send, fx_recv,
    gx_send, gx_recv, ob_send, ob_recv, fs_sem, out_sem,
):
    dp = lax.axis_index("dp")
    tn = lax.axis_index("tensor")
    x, z = dp // 4, dp % 4
    core = tn % 2
    sib = tn + 1 - 2 * core
    sends = []

    def remote(src, dst, ssem, rsem, to, kept=sends):
        c = pltpu.make_async_remote_copy(
            src_ref=src, dst_ref=dst, send_sem=ssem, recv_sem=rsem,
            device_id=to, device_id_type=MESH,
        )
        c.start()
        kept.append(c)

    def arrived(ref, ssem, rsem):
        pltpu.make_async_remote_copy(
            src_ref=ref, dst_ref=ref, send_sem=ssem, recv_sem=rsem,
            device_id=(dp, tn), device_id_type=MESH,
        ).wait_recv()

    def local(src, dst, k):
        c = pltpu.make_async_copy(src, dst, loc_sem.at[k])
        c.start()
        return c

    own_rows = pl.multiple_of(core * CH, CH)
    sib_rows = pl.multiple_of(CH - core * CH, CH)
    own_lanes = pl.multiple_of(core * LANES, LANES)
    sib_lanes = pl.multiple_of(LANES - core * LANES, LANES)
    ld_w = local(out_w.at[:, pl.ds(own_lanes, LANES)], W.at[dp, pl.ds(own_rows, CH)], 0)
    ld_pool = local(pool, PL, 1)
    ld_x = local(conv_in, XN, 2)
    ld_siw = local(step_in_w, SIW, 3)
    ld_sw = local(step_w, SWV, 4)
    ld_g = local(gate_in, GN, 5)

    bar = pltpu.get_barrier_semaphore()
    for d in range(1, 16):
        pl.semaphore_signal(bar, inc=1, device_id=((dp + d) % 16, tn), device_id_type=MESH)
    for d in range(1, 8):
        pl.semaphore_signal(bar, inc=1, device_id=(dp, (tn + d) % 8), device_id_type=MESH)

    row16 = iota((16, LANES), 0)
    lane16 = iota((16, LANES), 1)
    spread16 = (lane16 % 16 == row16).astype(F32).astype(BF16)

    def along_lanes(listed):
        wide = dot(listed.astype(F32).astype(BF16), spread16)
        wide = jnp.where(iota((SESS, LANES), 0) == iota((SESS, LANES), 1) // 16, wide, 0.0)
        return jnp.sum(wide, axis=0, keepdims=True).astype(jnp.int32)

    slot = along_lanes(page_slot[...])
    lane = iota((1, LANES), 1)
    owner = along_lanes(page_owner[:, 0, :])
    owner = jnp.where(lane < 96, owner, 16)
    count = jnp.zeros((1, LANES), jnp.int32)
    for s in range(SESS):
        count = jnp.where(lane // 16 == s, page_count[s], count)
    stored = (lane % 16 < count).astype(jnp.int32)
    own_hot = (owner == iota((16, LANES), 0)).astype(F32)
    before = (iota((LANES, LANES), 0) < iota((LANES, LANES), 1)).astype(F32).astype(BF16)
    ahead = dot(own_hot.astype(BF16), before)
    rank = jnp.sum(own_hot * ahead, axis=0, keepdims=True).astype(jnp.int32)
    ask_row = jnp.where(stored > 0, owner * 16 + rank, -1)
    got_row = jnp.where(stored > 0, jnp.where(rank < 8, owner * 8 + rank, LANES + owner), -1)
    row_io = iota((256, LANES), 0)
    ask = (ask_row == row_io).astype(F32).astype(BF16)
    slot_hot = (iota((LANES, LANES), 0) == slot).astype(F32).astype(BF16)
    REQ[...] = dot_nt(ask, slot_hot).astype(BF16).reshape(16, 16, LANES)
    for p in range(CB):
        cols = slice(p * LANES, (p + 1) * LANES)
        SPB[pl.ds(p, KW, stride=CB), :] = conv_w[:, cols]
        SPB[pl.ds(4 * CB + p, 1), :] = conv_b[:, cols]
        SPB[pl.ds(5 * CB + p, 1), :] = skip[:, cols]
        SPB[pl.ds(8 * CB + p, NS, stride=CB), :] = -LOG2E * jnp.exp(decay_log[:, cols])
    CPW[...] = jnp.zeros_like(CPW)
    CPW[0 : 2 * NS, :] = coup_w[...]
    RSS[ROWS:, :] = jnp.zeros((PADDED - ROWS, PW), BF16)

    EB[...] = (iota((LANES, 2 * NS * LANES), 0) == iota((LANES, 2 * NS * LANES), 1) // LANES).astype(
        F32
    ).astype(BF16)
    pl.semaphore_wait(bar, 22)

    def part_rows(q, p):
        base = own_rows if q == 0 else sib_rows
        return pl.ds(pl.multiple_of(base + p * QR, QR), QR)

    def dp_of(q, a, b):
        return a * 4 + b if q == 0 else b * 4 + a

    def coords(q):
        return (x, z) if q == 0 else (z, x)

    def part(q, da, db, p):
        a, b = coords(q)
        return W.at[dp_of(q, (a + 4 - da) % 4, (b + 4 - db) % 4), part_rows(q, p)]

    def gather_step(label):
        q, da, db, p = label
        a, b = coords(q)
        ref = part(q, da, db, p)
        if (da, db) != (0, 0):
            k = gather_label(*label)
            arrived(ref, ag_send.at[k], ag_recv.at[k])
        elif q == 1:
            arrived(ref, sib_send.at[p], sib_recv.at[p])
        for axis, step, nlabel in gather_forwards(*label):
            k = gather_label(*nlabel)
            to = ((a + step) % 4, b) if axis == "a" else (a, (b + step) % 4)
            remote(ref, ref, ag_send.at[k], ag_recv.at[k], (dp_of(q, *to), tn))

    events = gather_events()
    cursor = [0]

    def advance(upto):
        while cursor[0] < min(upto, len(events)):
            gather_step(events[cursor[0]])
            cursor[0] += 1

    for p in (0, 1):
        remote(
            out_w.at[pl.ds(p * QR, QR), pl.ds(sib_lanes, LANES)],
            W.at[dp, part_rows(0, p)], sib_send.at[p], sib_recv.at[p], (dp, sib),
        )

    RQIN[dp] = REQ[dp]
    for d in range(1, 16):
        to = (dp + d) % 16
        remote(REQ.at[to], RQIN.at[dp], rq_send.at[d], rq_recv.at[d], (to, tn))
    ld_w.wait()
    advance(2)
    got = (got_row == row_io).astype(F32).T[0:96, :].astype(BF16)


    ld_pool.wait()
    pool_low = PL[...].astype(BF16)

    def permute(e, _):
        pick = (iota((PAGE, LANES), 0) - ENT * iota((PAGE, LANES), 1) == e).astype(F32)
        PP[:, pl.ds(pl.multiple_of(e * LANES, LANES), LANES)] = dot(
            pool_low, pick.astype(BF16)
        ).astype(BF16)
        return 0

    lax.fori_loop(0, ENT, permute, 0)
    PP[:, ENT * LANES :] = jnp.zeros((LANES, LANES), BF16)

    for d in range(1, 16):
        src = (dp + 16 - d) % 16
        arrived(RQIN.at[src], rq_send.at[d], rq_recv.at[d])
    asked = RQIN[...].astype(F32)
    first8 = asked[:, 0:8, :].reshape(LANES, LANES).astype(BF16)
    low = dot(first8, PP[:, 0:HALF]).reshape(16, 8, HALF)
    high = dot(first8, PP[:, HALF : 2 * HALF]).reshape(16, 8, HALF)
    PS[...] = jnp.concatenate([low, high], axis=1).astype(BF16)
    ninth = dot(asked[:, 8, :].astype(BF16), PP[...])
    S8[...] = ninth.reshape(16, 1, 2 * HALF)
    PRV[dp] = PS[dp]
    P8[dp] = S8[dp]
    for d in range(1, 16):
        to = (dp + d) % 16
        remote(PS.at[to], PRV.at[dp], pa_send.at[d], pa_recv.at[d], (to, tn))
        remote(S8.at[to], P8.at[dp], pb_send.at[d], pb_recv.at[d], (to, tn))

    advance(4)

    ld_x.wait()

    def spread(g, _):
        r = pl.multiple_of(g * 16, 16)
        for p in range(CB):
            S2[pl.ds(g * 256 + p, 16, stride=CB), :] = XN[
                pl.ds(r, 16), p * LANES : (p + 1) * LANES
            ].astype(F32)
        return 0

    lax.fori_loop(0, ROWS // 16, spread, 0)

    taps = [SPB[w * CB : (w + 1) * CB, :] for w in range(KW)]
    bias = SPB[4 * CB : 5 * CB, :]
    none = jnp.zeros((CB, LANES), F32)
    for s in range(SESS):
        raw = [S2[(s * NEW + t) * CB : (s * NEW + t + 1) * CB, :] for t in range(3)]
        for t in range(3):
            pre = bias
            for u in range(t + 1):
                pre = pre + taps[3 - t + u] * raw[u]
            PRE[(s * 3 + t) * CB : (s * 3 + t + 1) * CB, :] = pre

    def conv_session(s, _):
        def step(i, hist):
            h3, h2, h1 = hist
            for u in range(8):
                at = pl.ds(pl.multiple_of((s * NEW + i * 8 + u) * CB, CB), CB)
                now = S2[at, :]
                pre = bias + taps[0] * h3 + taps[1] * h2 + taps[2] * h1 + taps[3] * now
                S2[at, :] = pre * sigmoid(pre)
                h3, h2, h1 = h2, h1, now
            return (h3, h2, h1)

        lax.fori_loop(0, NEW // 8, step, (none, none, none))
        return 0

    def collect(g, _):
        r = pl.multiple_of(g * 16, 16)
        for p in range(CB):
            XN[pl.ds(r, 16), p * LANES : (p + 1) * LANES] = S2[
                pl.ds(g * 256 + p, 16, stride=CB), :
            ].astype(BF16)
        return 0

    ld_siw.wait()

    def project(m, _):
        r = pl.ds(pl.multiple_of(m * 96, 96), 96)
        RSS[r, 0:RANK] = dot(XN[r, :], SIW[...]).astype(BF16)
        RSS[r, RANK:] = dot_nt(XN[r, :], CPW[...]).astype(BF16)
        return 0

    def prepare(group):
        first, last = GROUPS[group]
        lax.fori_loop(first, last, conv_session, 0)
        lax.fori_loop(first * NEW // 16, last * NEW // 16, collect, 0)
        lax.fori_loop(first, last, project, 0)

    def share(group, who):
        base, rows = GROUP_ROWS[group]
        return pl.ds(pl.multiple_of(base + who * rows, 16), rows)

    def landing(group):
        return pl.ds(48 * group, GROUP_ROWS[group][1])

    def send_sums(group):
        for d in range(1, 8):
            to = (tn + d) % 8
            remote(
                RSS.at[share(group, to)], RSR.at[d, landing(group)],
                rs_send.at[group, d], rs_recv.at[group, d], (dp, to),
            )

    prepare(0)
    send_sums(0)
    advance(8)
    prepare(1)

    advance(8)

    for d in range(1, 16):
        src = (dp + 16 - d) % 16
        arrived(PRV.at[src], pa_send.at[d], pa_recv.at[d])
        arrived(P8.at[src], pb_send.at[d], pb_recv.at[d])

    for s in range(2):
        for o in range(16):
            RALL[o * 8 : o * 8 + 8, :] = PRV[o].astype(F32)[8 * s : 8 * s + 8, :]
        RALL[LANES : LANES + 16, :] = P8[...].reshape(16, 2 * HALF)[:, s * HALF : (s + 1) * HALF]
        RALL[LANES + 16 :, :] = jnp.zeros((LANES - 16, HALF), F32)
        FT[:, s * HALF : (s + 1) * HALF] = dot(got, RALL[...].astype(BF16))


    advance(8)

    F2[SESS * 3 * CB : FIX * CB, :] = jnp.zeros(((FIX - SESS * 3) * CB, LANES), F32)
    for s in range(SESS):
        hist = [
            FT[s * CB : (s + 1) * CB, (NS + w) * LANES : (NS + w + 1) * LANES] for w in range(3)
        ]
        for t in range(3):
            r = s * 3 + t
            pre = PRE[r * CB : (r + 1) * CB, :]
            for w in range(3 - t):
                pre = pre + taps[w] * hist[t + w]
            sg = pre * sigmoid(pre)
            S2[(s * NEW + t) * CB : (s * NEW + t + 1) * CB, :] = sg
            F2[r * CB : (r + 1) * CB, :] = sg
    for p in range(CB):
        XF[:, p * LANES : (p + 1) * LANES] = F2[pl.ds(p, FIX, stride=CB), :].astype(BF16)
    FXS[:, 0:RANK] = dot(XF[...], SIW[...]).astype(BF16)
    FXS[:, RANK:] = dot_nt(XF[...], CPW[...]).astype(BF16)
    for d in range(1, 8):
        to = (tn + d) % 8
        remote(FXS, FXR.at[d], fx_send.at[d], fx_recv.at[d], (dp, to))

    advance(8)

    def normalize(sums):
        low = sums[:, 0:RANK]
        inv_rms = lax.rsqrt(jnp.mean(low * low, axis=-1, keepdims=True) + EPSILON)
        return (low * inv_rms * step_gain[...]).astype(BF16), sums[:, RANK:].astype(BF16)

    an_sends = ([], [])

    def spread_normed(group):
        mine = share(group, tn)
        total = RSS[mine, :].astype(F32)
        for d in range(1, 8):
            ref = RSR.at[d, landing(group)]
            arrived(ref, rs_send.at[group, d], rs_recv.at[group, d])
            total = total + ref[...].astype(F32)
        AGB[mine, 0:RANK], AGB[mine, RANK:] = normalize(total)
        for d in range(1, 8):
            to = (tn + d) % 8
            remote(
                AGB.at[mine], AGB.at[mine], an_send.at[group, d], an_recv.at[group, d],
                (dp, to), an_sends[group],
            )

    def take_normed(group):
        for d in range(1, 8):
            src = (tn + 8 - d) % 8
            arrived(AGB.at[share(group, src)], an_send.at[group, d], an_recv.at[group, d])
        for c in an_sends[group]:
            c.wait_send()

    spread_normed(0)
    send_sums(1)
    advance(12)
    take_normed(0)

    fixed = FXS[...].astype(F32)
    for d in range(1, 8):
        arrived(FXR.at[d], fx_send.at[d], fx_recv.at[d])
        fixed = fixed + FXR[d].astype(F32)
    normed, coupled = normalize(fixed)
    place = iota((96, FIX), 0)
    place = ((place % 16 < 3) & (place // 16 * 3 + place % 16 == iota((96, FIX), 1))).astype(F32)
    FXP[...] = dot(place.astype(BF16), jnp.concatenate([normed, coupled], axis=1))

    def correct(group):
        for s in range(*GROUPS[group]):
            r = slice(s * NEW, s * NEW + 16)
            AGB[r, :] = jnp.where(
                iota((16, PW), 0) < 3, FXP[s * 16 : s * 16 + 16, :], AGB[r, :].astype(F32)
            ).astype(BF16)

    correct(0)
    advance(16)

    ld_sw.wait()

    def step_size(m, _):
        r = pl.ds(pl.multiple_of(m * 96, 96), 96)
        for p in range(0, CB, 2):
            cols = slice(p * LANES, (p + 2) * LANES)
            v = dot(AGB[r, 0:RANK], SWV[:, cols]) + step_b[:, cols]
            v = jnp.maximum(v, 0.0) + jnp.log1p(jnp.exp(-jnp.abs(v)))
            for i in (0, 1):
                D2[pl.ds(m * 96 * CB + p + i, 96, stride=CB), :] = v[:, i * LANES : (i + 1) * LANES]
        return 0

    lax.fori_loop(*GROUPS[0], step_size, 0)
    advance(18)

    def gates(first, last):
        for s in range(first, last):
            arrived(G.at[1 - core, pl.ds(s * NEW, NEW)], gx_send.at[s], gx_recv.at[s])

    last_event = {}
    for i, (q, da, db, p) in enumerate(events):
        last_event[(da, db) if q == 0 else (db, da)] = i

    def multiply(pair, halves):
        advance(max(last_event[key] for key in pair) + 1)
        blocks = [((x + 4 - dx) % 4) * 4 + (z + 4 - dz) % 4 for dx, dz in pair]
        r = slice(halves[0] * HROWS, (halves[-1] + 1) * HROWS)

        def weight(k):
            return jnp.concatenate([W[b, k * CH : (k + 1) * CH, :] for b in blocks], axis=1)

        v = dot(G[0, r, :], weight(0)) + dot(G[1, r, :], weight(1))
        for i, b in enumerate(blocks):
            to, side = b // 2, b % 2
            OB[b, r, :] = v[:, i * LANES : (i + 1) * LANES].astype(BF16)

            @pl.when(to != tn)
            def _(b=b, to=to, side=side):
                for g in halves:
                    rg = pl.ds(g * HROWS, HROWS)
                    pltpu.make_async_remote_copy(
                        src_ref=OB.at[b, rg], dst_ref=RBO.at[tn, side, rg],
                        send_sem=ob_send.at[b, g], recv_sem=ob_recv.at[tn, side, g],
                        device_id=(dp, to), device_id_type=MESH,
                    ).start()

            @pl.when(to == tn)
            def _(b=b, side=side, r=r):
                RBO[tn, side, r, :] = OB[b, r, :]

    ld_g.wait()
    outs = []
    for s in range(SESS):
        if s == 1:
            spread_normed(1)
        if s == GROUPS[1][0]:
            take_normed(1)
            correct(1)
            lax.fori_loop(*GROUPS[1], step_size, 0)
        both = dot(AGB[s * NEW : (s + 1) * NEW, RANK:], EB[...])
        for n in range(2 * NS):
            BC[n * NEW : (n + 1) * NEW, :] = both[:, n * LANES : (n + 1) * LANES]
        for h in (0, 1):
            rate = [SPB[(8 + n) * CB + 8 * h : (8 + n) * CB + 8 * h + 8, :] for n in range(NS)]
            direct = SPB[5 * CB + 8 * h : 5 * CB + 8 * h + 8, :]
            start = tuple(
                FT[s * CB + 8 * h : s * CB + 8 * h + 8, n * LANES : (n + 1) * LANES]
                for n in range(NS)
            )

            def token(i, state, h=h, s=s, rate=rate, direct=direct):
                state = list(state)
                for u in range(8):
                    t = i * 8 + u
                    at = pl.ds(pl.multiple_of((s * NEW + t) * CB + 8 * h, 8), 8)
                    dt, sg = D2[at, :], S2[at, :]
                    dx = dt * sg
                    acc = [direct * sg, None]
                    for n in range(NS):
                        bn = BC[pl.ds(n * NEW + t, 8, stride=0), :]
                        cn = BC[pl.ds((NS + n) * NEW + t, 8, stride=0), :]
                        state[n] = jnp.exp2(dt * rate[n]) * state[n] + dx * bn
                        term = cn * state[n]
                        acc[n % 2] = term if acc[n % 2] is None else acc[n % 2] + term
                    S2[at, :] = acc[0] + acc[1]
                return tuple(state)

            last = lax.fori_loop(0, NEW // 8, token, start)
            advance(18 + (22 * (2 * s + h + 1)) // 12)
            for n in range(NS):
                FSB[n * CB + 8 * h : n * CB + 8 * h + 8, :] = last[n]
        for p in range(CB):
            FSV[s, :, p * LANES : (p + 1) * LANES] = FSB[pl.ds(p, NS, stride=CB), :]
        c = pltpu.make_async_copy(FSV.at[s], final_state.at[s], fs_sem.at[s])
        c.start()
        outs.append(c)

        def gate(g, _, s=s):
            r = pl.ds(pl.multiple_of(s * NEW + g * 16, 16), 16)
            for p in range(CB):
                cols = slice(p * LANES, (p + 1) * LANES)
                gt = GN[r, cols].astype(F32)
                y = S2[pl.ds((s * NEW + g * 16) * CB + p, 16, stride=CB), :]
                G[core, r, cols] = (y * (gt * sigmoid(gt))).astype(BF16)
            return 0

        lax.fori_loop(0, NEW // 16, gate, 0)
        here = G.at[core, pl.ds(s * NEW, NEW)]
        remote(here, here, gx_send.at[s], gx_recv.at[s], (dp, sib))
        if s in EARLY:
            if s == SESS // 2 - 1:
                gates(0, s + 1)
            for pair in PAIRS[slice(*EARLY[s])]:
                multiply(pair, (0,))

    advance(48)
    gates(SESS // 2, SESS)
    for k, pair in enumerate(PAIRS):
        multiply(pair, (1,) if k < SOON else (0, 1))
    advance(len(events))

    for side in (1 - z % 2, z % 2):
        for g in (0, 1):
            rg = pl.ds(g * HROWS, HROWS)
            for d in range(1, 8):
                src = (tn + 8 - d) % 8
                arrived(RBO.at[src, side, rg], ob_send.at[0, g], ob_recv.at[src, side, g])
            for c in (0, 1):

                def finish(m, _, c=c, g=g, side=side):
                    r = pl.ds(pl.multiple_of(g * HROWS + m * 96, 32), 96)
                    v = RBO[c, side, r, :].astype(F32)
                    for y in range(1, 4):
                        v = v + RBO[2 * y + c, side, r, :].astype(F32)
                    at = pl.multiple_of(side * 256 + c * LANES, LANES)
                    OUTV[r, pl.ds(at, LANES)] = v.astype(BF16)
                    return 0

                lax.fori_loop(0, HROWS // 96, finish, 0)
            cols = pl.ds(pl.multiple_of(side * 256, 256), 256)
            c = pltpu.make_async_copy(
                OUTV.at[rg, cols], mixer_out.at[rg, cols], out_sem.at[side, g]
            )
            c.start()
            outs.append(c)
    for src in range(16):

        @pl.when(src // 2 != tn)
        def _(src=src):
            for g in (0, 1):
                ref = OB.at[src, pl.ds(g * HROWS, HROWS)]
                pltpu.make_async_remote_copy(
                    src_ref=ref, dst_ref=ref, send_sem=ob_send.at[src, g],
                    recv_sem=ob_recv.at[0, 0, 0], device_id=(dp, tn), device_id_type=MESH,
                ).wait_send()

    for c in sends:
        c.wait_send()
    for c in outs:
        c.wait()


def settle(mixer_in, state_in, mixer_out, state_out, mixer, state, sems):
    hops = []
    for i, (src, via, dst) in enumerate(
        ((state_in, state, state_out), (mixer_in, mixer, mixer_out))
    ):
        for s in range(0, SESS, 2):
            part = pl.ds(s, 2)
            first = pltpu.make_async_copy(src.at[part], via.at[part], sems.at[0, i, s])
            last = pltpu.make_async_copy(via.at[part], dst.at[part], sems.at[1, i, s])
            first.start()
            hops.append((first, last))
    for first, last in hops:
        first.wait()
        last.start()
    for first, last in hops:
        last.wait()


def body(
    conv_input, gate_input, conv_weight, conv_bias, state_pool, page_owner, page_slot, page_count,
    step_in_weight, coupling_weight, step_gain, step_weight, step_bias, decay_log, skip_gain,
    out_weight,
):
    vmem = pl.BlockSpec(memory_space=pltpu.VMEM)
    hbm = pl.BlockSpec(memory_space=pl.ANY)
    sem = pltpu.SemaphoreType.DMA
    mixer_out, final_state = pl.pallas_call(
        kernel,
        out_shape=(
            jax.ShapeDtypeStruct((ROWS, 512), BF16),
            jax.ShapeDtypeStruct((SESS, NS, CH), F32),
        ),
        in_specs=[vmem] * 2 + [pl.BlockSpec(memory_space=pltpu.SMEM)] + [vmem] * 7 + [hbm] * 6,
        out_specs=(hbm, hbm),
        scratch_shapes=[
            pltpu.VMEM((16, 2 * CH, LANES), BF16),
            pltpu.VMEM((2, ROWS, CH), BF16),
            pltpu.VMEM((ROWS, CH), BF16),
            pltpu.VMEM((ROWS, CH), BF16),
            pltpu.VMEM((CH, RANK), BF16),
            pltpu.VMEM((RANK, CH), BF16),
            pltpu.VMEM((ROWS * CB + 16, LANES), F32),
            pltpu.VMEM((ROWS * CB + 16, LANES), F32),
            pltpu.VMEM((LANES, PAGE), F32),
            pltpu.VMEM((LANES, 2 * HALF), BF16),
            pltpu.VMEM((16, 16, LANES), BF16),
            pltpu.VMEM((16, 16, LANES), BF16),
            pltpu.VMEM((16, 16, HALF), BF16),
            pltpu.VMEM((16, 16, HALF), BF16),
            pltpu.VMEM((16, 1, 2 * HALF), F32),
            pltpu.VMEM((16, 1, 2 * HALF), F32),
            pltpu.VMEM((256, HALF), F32),
            pltpu.VMEM((96, 2 * HALF), F32),
            pltpu.VMEM((SESS * 3 * CB, LANES), F32),
            pltpu.VMEM((FIX * CB + 16, LANES), F32),
            pltpu.VMEM((FIX, CH), BF16),
            pltpu.VMEM((FIX, PW), BF16),
            pltpu.VMEM((8, FIX, PW), BF16),
            pltpu.VMEM((24 * CB + 16, LANES), F32),
            pltpu.VMEM((LANES, CH), BF16),
            pltpu.VMEM((PADDED, PW), BF16),
            pltpu.VMEM((8, 80, PW), BF16),
            pltpu.VMEM((PADDED, PW), BF16),
            pltpu.VMEM((96, PW), F32),
            pltpu.VMEM((LANES, 2 * NS * LANES), BF16),
            pltpu.VMEM((2 * NS * NEW + 8, LANES), F32),
            pltpu.VMEM((NS * CB + 16, LANES), F32),
            pltpu.VMEM((SESS, NS, CH), F32),
            pltpu.VMEM((16, ROWS, LANES), BF16),
            pltpu.VMEM((8, 2, ROWS, LANES), BF16),
            pltpu.VMEM((ROWS, 512), BF16),
            sem((6,)), sem((64,)), sem((64,)), sem((2,)), sem((2,)), sem((16,)), sem((16,)),
            sem((16,)), sem((16,)), sem((16,)), sem((16,)), sem((2, 8)), sem((2, 8)),
            sem((2, 8)), sem((2, 8)), sem((8,)), sem((8,)),
            sem((SESS,)), sem((SESS,)), sem((16, 2)), sem((8, 2, 2)), sem((SESS,)), sem((2, 2)),
        ],
        compiler_params=pltpu.CompilerParams(
            collective_id=0, has_side_effects=True, vmem_limit_bytes=62 << 20
        ),
        cost_estimate=pl.CostEstimate(
            flops=2 * ROWS * CH * (4096 + 1056), bytes_accessed=12 << 20, transcendentals=20 << 20
        ),
    )(
        jnp.transpose(page_owner, (0, 2, 1)), page_slot, page_count,
        conv_weight, conv_bias.reshape(1, -1), coupling_weight, step_gain.reshape(1, -1),
        step_bias.reshape(1, -1), decay_log, skip_gain.reshape(1, -1),
        conv_input.reshape(ROWS, CH), gate_input.reshape(ROWS, CH), state_pool,
        step_in_weight, step_weight, out_weight,
    )
    mixer_out = mixer_out.reshape(SESS, NEW, 512)
    return pl.pallas_call(
        settle,
        out_shape=(
            jax.ShapeDtypeStruct(mixer_out.shape, BF16),
            jax.ShapeDtypeStruct(final_state.shape, F32),
        ),
        in_specs=[hbm, hbm],
        out_specs=(hbm, hbm),
        scratch_shapes=[
            pltpu.VMEM(mixer_out.shape, BF16), pltpu.VMEM(final_state.shape, F32), sem((2, 2, SESS)),
        ],
    )(mixer_out, final_state)


def solution(mesh):
    return jax.shard_map(
        body,
        mesh=mesh,
        in_specs=(
            P("dp", None, "tensor"),
            P("dp", None, "tensor"),
            P(None, "tensor"),
            P("tensor"),
            P("dp", "tensor"),
            P("dp", None, None),
            P("dp", None),
            P("dp"),
            P("tensor", None),
            P(None, "tensor"),
            P(),
            P(None, "tensor"),
            P("tensor"),
            P(None, "tensor"),
            P("tensor"),
            P("tensor", "dp"),
        ),
        out_specs=(P("dp", None, "tensor"), P("dp", None, "tensor")),
        check_vma=False,
    )
```

```python
import jax
import jax.numpy as jnp
from jax import lax
from jax.experimental import pallas as pl
from jax.experimental.pallas import tpu as pltpu
from jax.sharding import PartitionSpec as P

EPSILON = 1e-06
LOG2E = 1.4426950408889634
MESH = pl.DeviceIdType.MESH
F32 = jnp.float32
BF16 = jnp.bfloat16

SESS, NEW, ROWS = 6, 96, 576
CB, LANES, CH = 16, 128, 2048
NS, KW, RANK, ENT = 16, 4, 512, 19
PAGE = CH // CB * ENT
HALF = 10 * LANES
GROUPS = ((0, 4), (4, 6))
GROUP_ROWS = ((0, 48), (384, 32))
PADDED = 640
PW = RANK + LANES
FIX = 32
QR = 1024


def gather_label(q, da, db, p):
    return ((q * 4 + da) * 4 + db) * 2 + p


def gather_events():
    return [
        (0, 0, 0, 0), (0, 0, 0, 1), (1, 0, 0, 0), (1, 0, 0, 1),
        (0, 0, 1, 0), (0, 0, 3, 0), (0, 1, 0, 0), (0, 3, 0, 0),
        (0, 0, 3, 1), (0, 0, 1, 1), (0, 1, 0, 1), (0, 3, 0, 1),
        (1, 1, 0, 0), (1, 0, 3, 0), (1, 0, 1, 0), (1, 3, 0, 0),
        (1, 0, 3, 1), (1, 0, 1, 1), (1, 3, 0, 1), (1, 1, 0, 1),
        (0, 1, 3, 0), (0, 2, 0, 0), (0, 2, 0, 1), (0, 0, 2, 0),
        (0, 1, 1, 0), (0, 3, 3, 0), (1, 1, 3, 0), (1, 1, 1, 0),
        (0, 3, 1, 0), (1, 3, 3, 0), (1, 0, 2, 0), (0, 0, 2, 1),
        (1, 3, 1, 0), (0, 1, 1, 1), (0, 1, 3, 1), (1, 0, 2, 1),
        (1, 3, 1, 1), (1, 3, 3, 1), (0, 3, 1, 1), (0, 3, 3, 1),
        (1, 1, 1, 1), (1, 1, 3, 1), (1, 2, 0, 1), (1, 2, 0, 0),
        (0, 2, 1, 0), (0, 2, 3, 0), (1, 1, 2, 0), (1, 3, 2, 1),
        (0, 2, 1, 1), (0, 2, 3, 1), (1, 3, 2, 0), (1, 1, 2, 1),
        (1, 2, 3, 1), (1, 2, 1, 1), (0, 1, 2, 1), (0, 1, 2, 0),
        (1, 2, 1, 0), (1, 2, 3, 0), (0, 3, 2, 1), (0, 3, 2, 0),
        (0, 2, 2, 0), (0, 2, 2, 1), (1, 2, 2, 1), (1, 2, 2, 0),
    ]


PAIRS = (
    ((0, 0), (0, 1)), ((0, 3), (1, 0)), ((3, 0), (2, 0)), ((1, 3), (3, 3)),
    ((1, 1), (3, 1)), ((0, 2), (2, 1)), ((2, 3), (1, 2)), ((3, 2),), ((2, 2),),
)
EARLY = {2: (0, 2), 4: (2, 4)}
SOON = 4
HROWS = ROWS // 2


def gather_forwards(q, da, db, p):
    out = []
    if db == 0:
        if da == 0:
            out += [("a", 1, (q, 1, 0, p)), ("a", 3, (q, 3, 0, p))]
        if da == 1 and p == 0:
            out.append(("a", 1, (q, 2, 0, 0)))
        if da == 3 and p == 1:
            out.append(("a", 3, (q, 2, 0, 1)))
        out += [("b", 1, (q, da, 1, p)), ("b", 3, (q, da, 3, p))]
    else:
        if db == 1 and p == 0:
            out.append(("b", 1, (q, da, 2, 0)))
        if db == 3 and p == 1:
            out.append(("b", 3, (q, da, 2, 1)))
    return out


def sigmoid(v):
    return 0.5 * (1.0 + jnp.tanh(0.5 * v))


def dot_nt(a, b):
    return lax.dot_general(a, b, (((1,), (1,)), ((), ())), preferred_element_type=F32)


def dot(a, b):
    return jnp.dot(a, b, preferred_element_type=F32)


def iota(shape, dim):
    return lax.broadcasted_iota(jnp.int32, shape, dim)


def kernel(
    page_owner, page_slot, page_count, conv_w, conv_b, coup_w, step_gain, step_b, decay_log, skip,
    conv_in, gate_in, pool, step_in_w, step_w, out_w,
    mixer_out, final_state,
    W, G, XN, GN, SIW, SWV, S2, D2, PL, PP, REQ, RQIN, PS, PRV, S8, P8, RALL, FT,
    PRE, F2, XF, FXS, FXR,
    SPB, CPW, RSS, RSR, AGB, FXP, EB, BC, FSB, FSV, OB, RBO, OUTV,
    loc_sem, ag_send, ag_recv, sib_send, sib_recv, rq_send, rq_recv,
    pa_send, pa_recv, pb_send, pb_recv, rs_send, rs_recv, an_send, an_recv, fx_send, fx_recv,
    gx_send, gx_recv, ob_send, ob_recv, fs_sem, out_sem,
):
    dp = lax.axis_index("dp")
    tn = lax.axis_index("tensor")
    x, z = dp // 4, dp % 4
    core = tn % 2
    sib = tn + 1 - 2 * core
    sends = []

    def remote(src, dst, ssem, rsem, to, kept=sends):
        c = pltpu.make_async_remote_copy(
            src_ref=src, dst_ref=dst, send_sem=ssem, recv_sem=rsem,
            device_id=to, device_id_type=MESH,
        )
        c.start()
        kept.append(c)

    def arrived(ref, ssem, rsem):
        pltpu.make_async_remote_copy(
            src_ref=ref, dst_ref=ref, send_sem=ssem, recv_sem=rsem,
            device_id=(dp, tn), device_id_type=MESH,
        ).wait_recv()

    def local(src, dst, k):
        c = pltpu.make_async_copy(src, dst, loc_sem.at[k])
        c.start()
        return c

    own_rows = pl.multiple_of(core * CH, CH)
    sib_rows = pl.multiple_of(CH - core * CH, CH)
    own_lanes = pl.multiple_of(core * LANES, LANES)
    sib_lanes = pl.multiple_of(LANES - core * LANES, LANES)
    ld_w = local(out_w.at[:, pl.ds(own_lanes, LANES)], W.at[dp, pl.ds(own_rows, CH)], 0)
    ld_pool = local(pool, PL, 1)
    ld_x = local(conv_in, XN, 2)
    ld_siw = local(step_in_w, SIW, 3)
    ld_sw = local(step_w, SWV, 4)
    ld_g = local(gate_in, GN, 5)

    bar = pltpu.get_barrier_semaphore()
    for d in range(1, 16):
        pl.semaphore_signal(bar, inc=1, device_id=((dp + d) % 16, tn), device_id_type=MESH)
    for d in range(1, 8):
        pl.semaphore_signal(bar, inc=1, device_id=(dp, (tn + d) % 8), device_id_type=MESH)

    row16 = iota((16, LANES), 0)
    lane16 = iota((16, LANES), 1)
    spread16 = (lane16 % 16 == row16).astype(F32).astype(BF16)

    def along_lanes(listed):
        wide = dot(listed.astype(F32).astype(BF16), spread16)
        wide = jnp.where(iota((SESS, LANES), 0) == iota((SESS, LANES), 1) // 16, wide, 0.0)
        return jnp.sum(wide, axis=0, keepdims=True).astype(jnp.int32)

    slot = along_lanes(page_slot[...])
    lane = iota((1, LANES), 1)
    owner = along_lanes(page_owner[:, 0, :])
    owner = jnp.where(lane < 96, owner, 16)
    count = jnp.zeros((1, LANES), jnp.int32)
    for s in range(SESS):
        count = jnp.where(lane // 16 == s, page_count[s], count)
    stored = (lane % 16 < count).astype(jnp.int32)
    own_hot = (owner == iota((16, LANES), 0)).astype(F32)
    before = (iota((LANES, LANES), 0) < iota((LANES, LANES), 1)).astype(F32).astype(BF16)
    ahead = dot(own_hot.astype(BF16), before)
    rank = jnp.sum(own_hot * ahead, axis=0, keepdims=True).astype(jnp.int32)
    ask_row = jnp.where(stored > 0, owner * 16 + rank, -1)
    got_row = jnp.where(stored > 0, jnp.where(rank < 8, owner * 8 + rank, LANES + owner), -1)
    row_io = iota((256, LANES), 0)
    ask = (ask_row == row_io).astype(F32).astype(BF16)
    slot_hot = (iota((LANES, LANES), 0) == slot).astype(F32).astype(BF16)
    REQ[...] = dot_nt(ask, slot_hot).astype(BF16).reshape(16, 16, LANES)
    for p in range(CB):
        cols = slice(p * LANES, (p + 1) * LANES)
        SPB[pl.ds(p, KW, stride=CB), :] = conv_w[:, cols]
        SPB[pl.ds(4 * CB + p, 1), :] = conv_b[:, cols]
        SPB[pl.ds(5 * CB + p, 1), :] = skip[:, cols]
        SPB[pl.ds(8 * CB + p, NS, stride=CB), :] = -LOG2E * jnp.exp(decay_log[:, cols])
    CPW[...] = jnp.zeros_like(CPW)
    CPW[0 : 2 * NS, :] = coup_w[...]
    RSS[ROWS:, :] = jnp.zeros((PADDED - ROWS, PW), BF16)

    EB[...] = (iota((LANES, 2 * NS * LANES), 0) == iota((LANES, 2 * NS * LANES), 1) // LANES).astype(
        F32
    ).astype(BF16)
    pl.semaphore_wait(bar, 22)

    def part_rows(q, p):
        base = own_rows if q == 0 else sib_rows
        return pl.ds(pl.multiple_of(base + p * QR, QR), QR)

    def dp_of(q, a, b):
        return a * 4 + b if q == 0 else b * 4 + a

    def coords(q):
        return (x, z) if q == 0 else (z, x)

    def part(q, da, db, p):
        a, b = coords(q)
        return W.at[dp_of(q, (a + 4 - da) % 4, (b + 4 - db) % 4), part_rows(q, p)]

    def gather_step(label):
        q, da, db, p = label
        a, b = coords(q)
        ref = part(q, da, db, p)
        if (da, db) != (0, 0):
            k = gather_label(*label)
            arrived(ref, ag_send.at[k], ag_recv.at[k])
        elif q == 1:
            arrived(ref, sib_send.at[p], sib_recv.at[p])
        for axis, step, nlabel in gather_forwards(*label):
            k = gather_label(*nlabel)
            to = ((a + step) % 4, b) if axis == "a" else (a, (b + step) % 4)
            remote(ref, ref, ag_send.at[k], ag_recv.at[k], (dp_of(q, *to), tn))

    events = gather_events()
    cursor = [0]

    def advance(upto):
        while cursor[0] < min(upto, len(events)):
            gather_step(events[cursor[0]])
            cursor[0] += 1

    for p in (0, 1):
        remote(
            out_w.at[pl.ds(p * QR, QR), pl.ds(sib_lanes, LANES)],
            W.at[dp, part_rows(0, p)], sib_send.at[p], sib_recv.at[p], (dp, sib),
        )

    RQIN[dp] = REQ[dp]
    for d in range(1, 16):
        to = (dp + d) % 16
        remote(REQ.at[to], RQIN.at[dp], rq_send.at[d], rq_recv.at[d], (to, tn))
    ld_w.wait()
    advance(2)
    got = (got_row == row_io).astype(F32).T[0:96, :].astype(BF16)


    ld_pool.wait()
    pool_low = PL[...].astype(BF16)

    def permute(e, _):
        pick = (iota((PAGE, LANES), 0) - ENT * iota((PAGE, LANES), 1) == e).astype(F32)
        PP[:, pl.ds(pl.multiple_of(e * LANES, LANES), LANES)] = dot(
            pool_low, pick.astype(BF16)
        ).astype(BF16)
        return 0

    lax.fori_loop(0, ENT, permute, 0)
    PP[:, ENT * LANES :] = jnp.zeros((LANES, LANES), BF16)

    for d in range(1, 16):
        src = (dp + 16 - d) % 16
        arrived(RQIN.at[src], rq_send.at[d], rq_recv.at[d])
    asked = RQIN[...].astype(F32)
    first8 = asked[:, 0:8, :].reshape(LANES, LANES).astype(BF16)
    low = dot(first8, PP[:, 0:HALF]).reshape(16, 8, HALF)
    high = dot(first8, PP[:, HALF : 2 * HALF]).reshape(16, 8, HALF)
    PS[...] = jnp.concatenate([low, high], axis=1).astype(BF16)
    ninth = dot(asked[:, 8, :].astype(BF16), PP[...])
    S8[...] = ninth.reshape(16, 1, 2 * HALF)
    PRV[dp] = PS[dp]
    P8[dp] = S8[dp]
    for d in range(1, 16):
        to = (dp + d) % 16
        remote(PS.at[to], PRV.at[dp], pa_send.at[d], pa_recv.at[d], (to, tn))
        remote(S8.at[to], P8.at[dp], pb_send.at[d], pb_recv.at[d], (to, tn))

    advance(4)

    ld_x.wait()

    def spread(g, _):
        r = pl.multiple_of(g * 16, 16)
        for p in range(CB):
            S2[pl.ds(g * 256 + p, 16, stride=CB), :] = XN[
                pl.ds(r, 16), p * LANES : (p + 1) * LANES
            ].astype(F32)
        return 0

    lax.fori_loop(0, ROWS // 16, spread, 0)

    taps = [SPB[w * CB : (w + 1) * CB, :] for w in range(KW)]
    bias = SPB[4 * CB : 5 * CB, :]
    none = jnp.zeros((CB, LANES), F32)
    for s in range(SESS):
        raw = [S2[(s * NEW + t) * CB : (s * NEW + t + 1) * CB, :] for t in range(3)]
        for t in range(3):
            pre = bias
            for u in range(t + 1):
                pre = pre + taps[3 - t + u] * raw[u]
            PRE[(s * 3 + t) * CB : (s * 3 + t + 1) * CB, :] = pre

    def conv_session(s, _):
        def step(i, hist):
            h3, h2, h1 = hist
            for u in range(8):
                at = pl.ds(pl.multiple_of((s * NEW + i * 8 + u) * CB, CB), CB)
                now = S2[at, :]
                pre = bias + taps[0] * h3 + taps[1] * h2 + taps[2] * h1 + taps[3] * now
                S2[at, :] = pre * sigmoid(pre)
                h3, h2, h1 = h2, h1, now
            return (h3, h2, h1)

        lax.fori_loop(0, NEW // 8, step, (none, none, none))
        return 0

    def collect(g, _):
        r = pl.multiple_of(g * 16, 16)
        for p in range(CB):
            XN[pl.ds(r, 16), p * LANES : (p + 1) * LANES] = S2[
                pl.ds(g * 256 + p, 16, stride=CB), :
            ].astype(BF16)
        return 0

    ld_siw.wait()

    def project(m, _):
        r = pl.ds(pl.multiple_of(m * 96, 96), 96)
        RSS[r, 0:RANK] = dot(XN[r, :], SIW[...]).astype(BF16)
        RSS[r, RANK:] = dot_nt(XN[r, :], CPW[...]).astype(BF16)
        return 0

    def prepare(group):
        first, last = GROUPS[group]
        lax.fori_loop(first, last, conv_session, 0)
        lax.fori_loop(first * NEW // 16, last * NEW // 16, collect, 0)
        lax.fori_loop(first, last, project, 0)

    def share(group, who):
        base, rows = GROUP_ROWS[group]
        return pl.ds(pl.multiple_of(base + who * rows, 16), rows)

    def landing(group):
        return pl.ds(48 * group, GROUP_ROWS[group][1])

    def send_sums(group):
        for d in range(1, 8):
            to = (tn + d) % 8
            remote(
                RSS.at[share(group, to)], RSR.at[d, landing(group)],
                rs_send.at[group, d], rs_recv.at[group, d], (dp, to),
            )

    prepare(0)
    send_sums(0)
    advance(8)
    prepare(1)

    advance(8)

    for d in range(1, 16):
        src = (dp + 16 - d) % 16
        arrived(PRV.at[src], pa_send.at[d], pa_recv.at[d])
        arrived(P8.at[src], pb_send.at[d], pb_recv.at[d])

    for s in range(2):
        for o in range(16):
            RALL[o * 8 : o * 8 + 8, :] = PRV[o].astype(F32)[8 * s : 8 * s + 8, :]
        RALL[LANES : LANES + 16, :] = P8[...].reshape(16, 2 * HALF)[:, s * HALF : (s + 1) * HALF]
        RALL[LANES + 16 :, :] = jnp.zeros((LANES - 16, HALF), F32)
        FT[:, s * HALF : (s + 1) * HALF] = dot(got, RALL[...].astype(BF16))


    advance(8)

    F2[SESS * 3 * CB : FIX * CB, :] = jnp.zeros(((FIX - SESS * 3) * CB, LANES), F32)
    for s in range(SESS):
        hist = [
            FT[s * CB : (s + 1) * CB, (NS + w) * LANES : (NS + w + 1) * LANES] for w in range(3)
        ]
        for t in range(3):
            r = s * 3 + t
            pre = PRE[r * CB : (r + 1) * CB, :]
            for w in range(3 - t):
                pre = pre + taps[w] * hist[t + w]
            sg = pre * sigmoid(pre)
            S2[(s * NEW + t) * CB : (s * NEW + t + 1) * CB, :] = sg
            F2[r * CB : (r + 1) * CB, :] = sg
    for p in range(CB):
        XF[:, p * LANES : (p + 1) * LANES] = F2[pl.ds(p, FIX, stride=CB), :].astype(BF16)
    FXS[:, 0:RANK] = dot(XF[...], SIW[...]).astype(BF16)
    FXS[:, RANK:] = dot_nt(XF[...], CPW[...]).astype(BF16)
    for d in range(1, 8):
        to = (tn + d) % 8
        remote(FXS, FXR.at[d], fx_send.at[d], fx_recv.at[d], (dp, to))

    advance(8)

    def normalize(sums):
        low = sums[:, 0:RANK]
        inv_rms = lax.rsqrt(jnp.mean(low * low, axis=-1, keepdims=True) + EPSILON)
        return (low * inv_rms * step_gain[...]).astype(BF16), sums[:, RANK:].astype(BF16)

    an_sends = ([], [])

    def spread_normed(group):
        mine = share(group, tn)
        total = RSS[mine, :].astype(F32)
        for d in range(1, 8):
            ref = RSR.at[d, landing(group)]
            arrived(ref, rs_send.at[group, d], rs_recv.at[group, d])
            total = total + ref[...].astype(F32)
        AGB[mine, 0:RANK], AGB[mine, RANK:] = normalize(total)
        for d in range(1, 8):
            to = (tn + d) % 8
            remote(
                AGB.at[mine], AGB.at[mine], an_send.at[group, d], an_recv.at[group, d],
                (dp, to), an_sends[group],
            )

    def take_normed(group):
        for d in range(1, 8):
            src = (tn + 8 - d) % 8
            arrived(AGB.at[share(group, src)], an_send.at[group, d], an_recv.at[group, d])
        for c in an_sends[group]:
            c.wait_send()

    spread_normed(0)
    send_sums(1)
    advance(12)
    take_normed(0)

    fixed = FXS[...].astype(F32)
    for d in range(1, 8):
        arrived(FXR.at[d], fx_send.at[d], fx_recv.at[d])
        fixed = fixed + FXR[d].astype(F32)
    normed, coupled = normalize(fixed)
    place = iota((96, FIX), 0)
    place = ((place % 16 < 3) & (place // 16 * 3 + place % 16 == iota((96, FIX), 1))).astype(F32)
    FXP[...] = dot(place.astype(BF16), jnp.concatenate([normed, coupled], axis=1))

    def correct(group):
        for s in range(*GROUPS[group]):
            r = slice(s * NEW, s * NEW + 16)
            AGB[r, :] = jnp.where(
                iota((16, PW), 0) < 3, FXP[s * 16 : s * 16 + 16, :], AGB[r, :].astype(F32)
            ).astype(BF16)

    correct(0)
    advance(16)

    ld_sw.wait()

    def step_size(m, _):
        r = pl.ds(pl.multiple_of(m * 96, 96), 96)
        for p in range(0, CB, 2):
            cols = slice(p * LANES, (p + 2) * LANES)
            v = dot(AGB[r, 0:RANK], SWV[:, cols]) + step_b[:, cols]
            v = jnp.maximum(v, 0.0) + jnp.log1p(jnp.exp(-jnp.abs(v)))
            for i in (0, 1):
                D2[pl.ds(m * 96 * CB + p + i, 96, stride=CB), :] = v[:, i * LANES : (i + 1) * LANES]
        return 0

    lax.fori_loop(*GROUPS[0], step_size, 0)
    advance(18)

    def gates(first, last):
        for s in range(first, last):
            arrived(G.at[1 - core, pl.ds(s * NEW, NEW)], gx_send.at[s], gx_recv.at[s])

    last_event = {}
    for i, (q, da, db, p) in enumerate(events):
        last_event[(da, db) if q == 0 else (db, da)] = i

    def multiply(pair, halves):
        advance(max(last_event[key] for key in pair) + 1)
        blocks = [((x + 4 - dx) % 4) * 4 + (z + 4 - dz) % 4 for dx, dz in pair]
        r = slice(halves[0] * HROWS, (halves[-1] + 1) * HROWS)

        def weight(k):
            return jnp.concatenate([W[b, k * CH : (k + 1) * CH, :] for b in blocks], axis=1)

        v = dot(G[0, r, :], weight(0)) + dot(G[1, r, :], weight(1))
        for i, b in enumerate(blocks):
            to, side = b // 2, b % 2
            OB[b, r, :] = v[:, i * LANES : (i + 1) * LANES].astype(BF16)

            @pl.when(to != tn)
            def _(b=b, to=to, side=side):
                for g in halves:
                    rg = pl.ds(g * HROWS, HROWS)
                    pltpu.make_async_remote_copy(
                        src_ref=OB.at[b, rg], dst_ref=RBO.at[tn, side, rg],
                        send_sem=ob_send.at[b, g], recv_sem=ob_recv.at[tn, side, g],
                        device_id=(dp, to), device_id_type=MESH,
                    ).start()

            @pl.when(to == tn)
            def _(b=b, side=side, r=r):
                RBO[tn, side, r, :] = OB[b, r, :]

    ld_g.wait()
    outs = []
    for s in range(SESS):
        if s == 1:
            spread_normed(1)
        if s == GROUPS[1][0]:
            take_normed(1)
            correct(1)
            lax.fori_loop(*GROUPS[1], step_size, 0)
        both = dot(AGB[s * NEW : (s + 1) * NEW, RANK:], EB[...])
        for n in range(2 * NS):
            BC[n * NEW : (n + 1) * NEW, :] = both[:, n * LANES : (n + 1) * LANES]
        for h in (0, 1):
            rate = [SPB[(8 + n) * CB + 8 * h : (8 + n) * CB + 8 * h + 8, :] for n in range(NS)]
            direct = SPB[5 * CB + 8 * h : 5 * CB + 8 * h + 8, :]
            start = tuple(
                FT[s * CB + 8 * h : s * CB + 8 * h + 8, n * LANES : (n + 1) * LANES]
                for n in range(NS)
            )

            def token(i, state, h=h, s=s, rate=rate, direct=direct):
                state = list(state)
                for u in range(8):
                    t = i * 8 + u
                    at = pl.ds(pl.multiple_of((s * NEW + t) * CB + 8 * h, 8), 8)
                    dt, sg = D2[at, :], S2[at, :]
                    dx = dt * sg
                    acc = [direct * sg, None]
                    for n in range(NS):
                        bn = BC[pl.ds(n * NEW + t, 8, stride=0), :]
                        cn = BC[pl.ds((NS + n) * NEW + t, 8, stride=0), :]
                        state[n] = jnp.exp2(dt * rate[n]) * state[n] + dx * bn
                        term = cn * state[n]
                        acc[n % 2] = term if acc[n % 2] is None else acc[n % 2] + term
                    S2[at, :] = acc[0] + acc[1]
                return tuple(state)

            last = lax.fori_loop(0, NEW // 8, token, start)
            advance(18 + (22 * (2 * s + h + 1)) // 12)
            for n in range(NS):
                FSB[n * CB + 8 * h : n * CB + 8 * h + 8, :] = last[n]
        for p in range(CB):
            FSV[s, :, p * LANES : (p + 1) * LANES] = FSB[pl.ds(p, NS, stride=CB), :]
        c = pltpu.make_async_copy(FSV.at[s], final_state.at[s], fs_sem.at[s])
        c.start()
        outs.append(c)

        def gate(g, _, s=s):
            r = pl.ds(pl.multiple_of(s * NEW + g * 16, 16), 16)
            for p in range(CB):
                cols = slice(p * LANES, (p + 1) * LANES)
                gt = GN[r, cols].astype(F32)
                y = S2[pl.ds((s * NEW + g * 16) * CB + p, 16, stride=CB), :]
                G[core, r, cols] = (y * (gt * sigmoid(gt))).astype(BF16)
            return 0

        lax.fori_loop(0, NEW // 16, gate, 0)
        here = G.at[core, pl.ds(s * NEW, NEW)]
        remote(here, here, gx_send.at[s], gx_recv.at[s], (dp, sib))
        if s in EARLY:
            if s == SESS // 2 - 1:
                gates(0, s + 1)
            for pair in PAIRS[slice(*EARLY[s])]:
                multiply(pair, (0,))

    advance(50)
    gates(SESS // 2, SESS)
    for k, pair in enumerate(PAIRS):
        multiply(pair, (1,) if k < SOON else (0, 1))
    advance(len(events))

    for side in (1 - z % 2, z % 2):
        for g in (0, 1):
            rg = pl.ds(g * HROWS, HROWS)
            for d in range(1, 8):
                src = (tn + 8 - d) % 8
                arrived(RBO.at[src, side, rg], ob_send.at[0, g], ob_recv.at[src, side, g])
            for c in (0, 1):

                def finish(m, _, c=c, g=g, side=side):
                    r = pl.ds(pl.multiple_of(g * HROWS + m * 96, 32), 96)
                    v = RBO[c, side, r, :].astype(F32)
                    for y in range(1, 4):
                        v = v + RBO[2 * y + c, side, r, :].astype(F32)
                    at = pl.multiple_of(side * 256 + c * LANES, LANES)
                    OUTV[r, pl.ds(at, LANES)] = v.astype(BF16)
                    return 0

                lax.fori_loop(0, HROWS // 96, finish, 0)
            cols = pl.ds(pl.multiple_of(side * 256, 256), 256)
            c = pltpu.make_async_copy(
                OUTV.at[rg, cols], mixer_out.at[rg, cols], out_sem.at[side, g]
            )
            c.start()
            outs.append(c)
    for src in range(16):

        @pl.when(src // 2 != tn)
        def _(src=src):
            for g in (0, 1):
                ref = OB.at[src, pl.ds(g * HROWS, HROWS)]
                pltpu.make_async_remote_copy(
                    src_ref=ref, dst_ref=ref, send_sem=ob_send.at[src, g],
                    recv_sem=ob_recv.at[0, 0, 0], device_id=(dp, tn), device_id_type=MESH,
                ).wait_send()

    for c in sends:
        c.wait_send()
    for c in outs:
        c.wait()


def settle(mixer_in, state_in, mixer_out, state_out, mixer, state, sems):
    hops = []
    for i, (src, via, dst) in enumerate(
        ((state_in, state, state_out), (mixer_in, mixer, mixer_out))
    ):
        for s in range(0, SESS, 2):
            part = pl.ds(s, 2)
            first = pltpu.make_async_copy(src.at[part], via.at[part], sems.at[0, i, s])
            last = pltpu.make_async_copy(via.at[part], dst.at[part], sems.at[1, i, s])
            first.start()
            hops.append((first, last))
    for first, last in hops:
        first.wait()
        last.start()
    for first, last in hops:
        last.wait()


def body(
    conv_input, gate_input, conv_weight, conv_bias, state_pool, page_owner, page_slot, page_count,
    step_in_weight, coupling_weight, step_gain, step_weight, step_bias, decay_log, skip_gain,
    out_weight,
):
    vmem = pl.BlockSpec(memory_space=pltpu.VMEM)
    hbm = pl.BlockSpec(memory_space=pl.ANY)
    sem = pltpu.SemaphoreType.DMA
    mixer_out, final_state = pl.pallas_call(
        kernel,
        out_shape=(
            jax.ShapeDtypeStruct((ROWS, 512), BF16),
            jax.ShapeDtypeStruct((SESS, NS, CH), F32),
        ),
        in_specs=[vmem] * 2 + [pl.BlockSpec(memory_space=pltpu.SMEM)] + [vmem] * 7 + [hbm] * 6,
        out_specs=(hbm, hbm),
        scratch_shapes=[
            pltpu.VMEM((16, 2 * CH, LANES), BF16),
            pltpu.VMEM((2, ROWS, CH), BF16),
            pltpu.VMEM((ROWS, CH), BF16),
            pltpu.VMEM((ROWS, CH), BF16),
            pltpu.VMEM((CH, RANK), BF16),
            pltpu.VMEM((RANK, CH), BF16),
            pltpu.VMEM((ROWS * CB + 16, LANES), F32),
            pltpu.VMEM((ROWS * CB + 16, LANES), F32),
            pltpu.VMEM((LANES, PAGE), F32),
            pltpu.VMEM((LANES, 2 * HALF), BF16),
            pltpu.VMEM((16, 16, LANES), BF16),
            pltpu.VMEM((16, 16, LANES), BF16),
            pltpu.VMEM((16, 16, HALF), BF16),
            pltpu.VMEM((16, 16, HALF), BF16),
            pltpu.VMEM((16, 1, 2 * HALF), F32),
            pltpu.VMEM((16, 1, 2 * HALF), F32),
            pltpu.VMEM((256, HALF), F32),
            pltpu.VMEM((96, 2 * HALF), F32),
            pltpu.VMEM((SESS * 3 * CB, LANES), F32),
            pltpu.VMEM((FIX * CB + 16, LANES), F32),
            pltpu.VMEM((FIX, CH), BF16),
            pltpu.VMEM((FIX, PW), BF16),
            pltpu.VMEM((8, FIX, PW), BF16),
            pltpu.VMEM((24 * CB + 16, LANES), F32),
            pltpu.VMEM((LANES, CH), BF16),
            pltpu.VMEM((PADDED, PW), BF16),
            pltpu.VMEM((8, 80, PW), BF16),
            pltpu.VMEM((PADDED, PW), BF16),
            pltpu.VMEM((96, PW), F32),
            pltpu.VMEM((LANES, 2 * NS * LANES), BF16),
            pltpu.VMEM((2 * NS * NEW + 8, LANES), F32),
            pltpu.VMEM((NS * CB + 16, LANES), F32),
            pltpu.VMEM((SESS, NS, CH), F32),
            pltpu.VMEM((16, ROWS, LANES), BF16),
            pltpu.VMEM((8, 2, ROWS, LANES), BF16),
            pltpu.VMEM((ROWS, 512), BF16),
            sem((6,)), sem((64,)), sem((64,)), sem((2,)), sem((2,)), sem((16,)), sem((16,)),
            sem((16,)), sem((16,)), sem((16,)), sem((16,)), sem((2, 8)), sem((2, 8)),
            sem((2, 8)), sem((2, 8)), sem((8,)), sem((8,)),
            sem((SESS,)), sem((SESS,)), sem((16, 2)), sem((8, 2, 2)), sem((SESS,)), sem((2, 2)),
        ],
        compiler_params=pltpu.CompilerParams(
            collective_id=0, has_side_effects=True, vmem_limit_bytes=62 << 20
        ),
        cost_estimate=pl.CostEstimate(
            flops=2 * ROWS * CH * (4096 + 1056), bytes_accessed=12 << 20, transcendentals=20 << 20
        ),
    )(
        jnp.transpose(page_owner, (0, 2, 1)), page_slot, page_count,
        conv_weight, conv_bias.reshape(1, -1), coupling_weight, step_gain.reshape(1, -1),
        step_bias.reshape(1, -1), decay_log, skip_gain.reshape(1, -1),
        conv_input.reshape(ROWS, CH), gate_input.reshape(ROWS, CH), state_pool,
        step_in_weight, step_weight, out_weight,
    )
    mixer_out = mixer_out.reshape(SESS, NEW, 512)
    return pl.pallas_call(
        settle,
        out_shape=(
            jax.ShapeDtypeStruct(mixer_out.shape, BF16),
            jax.ShapeDtypeStruct(final_state.shape, F32),
        ),
        in_specs=[hbm, hbm],
        out_specs=(hbm, hbm),
        scratch_shapes=[
            pltpu.VMEM(mixer_out.shape, BF16), pltpu.VMEM(final_state.shape, F32), sem((2, 2, SESS)),
        ],
    )(mixer_out, final_state)


def solution(mesh):
    return jax.shard_map(
        body,
        mesh=mesh,
        in_specs=(
            P("dp", None, "tensor"),
            P("dp", None, "tensor"),
            P(None, "tensor"),
            P("tensor"),
            P("dp", "tensor"),
            P("dp", None, None),
            P("dp", None),
            P("dp"),
            P("tensor", None),
            P(None, "tensor"),
            P(),
            P(None, "tensor"),
            P("tensor"),
            P(None, "tensor"),
            P("tensor"),
            P("tensor", "dp"),
        ),
        out_specs=(P("dp", None, "tensor"), P("dp", None, "tensor")),
        check_vma=False,
    )
```
